256 devices in a mesh: section: 8 (over y, z_hi), dp: 32 (over z_lo, x, core).
Axes of the slice: x: 4, y: 4, z: 8 (z_hi: 2, z_lo: 4; z = z_hi * 4 + z_lo), core: 2. Of those that a mesh axis runs over, the one named last changes fastest.
Arguments:
- inputs: bfloat16 [32, 8, 16, 7168], P('dp')
- cotangent: bfloat16 [32, 8, 16, 7168], P('dp'), may hold values from -0.09375 to 0.09375
- send_memory: bfloat16 [8, 32, 8, 16, 7168], P('section', 'dp')
- recv_memory: bfloat16 [8, 32, 8, 16, 7168], P('section', 'dp')
- sample_ids: int32 [32, 8], P('dp'), may hold values from 0 to 7, each once within a row
- gains: bfloat16 [8, 2, 7168], P('section'), may hold values from 0.099609375 to 1.8984375
- down_weight: bfloat16 [8, 2, 7168, 64], P('section'), may hold values from -0.0625 to 0.0625
- up_weight: bfloat16 [8, 2, 64, 7168], P('section'), may hold values from -0.75 to 0.75
Outputs:
- grad_down: bfloat16 [8, 2, 7168, 64], P('section', None, 'dp')
- grad_up: bfloat16 [8, 2, 64, 7168], P('section', None, None, 'dp')
- grad_gain: bfloat16 [8, 2, 7168], P('section', None, 'dp')
The draws below stay inside these ranges and needn't reach their ends.
Inputs may be any that keep to these rules, and one draw needn't show every extreme that they name: `sample_ids`: each row names every slot 0 to 7 once.
All inputs are finite; a program needn't handle non-finite values.
Results may differ from the reference program's by a relative error of at most 0.035.
Values may be sent and summed in bfloat16 or wider, within the bound.
A program may use at most 128 MiB of HBM per device.

```python
import jax
import jax.numpy as jnp
from jax import lax

D = 7168
RANK = 64
LAYERS = 2
MICRO = 8
SEQ = 16
SECTIONS = 8
REPLICAS = 32


def rough_scales(key, full_shape, reach):
    first, second, third = jax.random.split(key, 3)
    row_scale = jnp.exp(jax.random.uniform(second, full_shape[:-1] + (1,), jnp.float32, -reach, reach))
    column_scale = jnp.exp(jax.random.uniform(third, (full_shape[-1],), jnp.float32, -reach, reach))
    return (first, row_scale * column_scale)


def rough_values(base_key, full_shape, factor_all):
    values = jax.random.normal(base_key, full_shape, jnp.float32)
    return values * factor_all


def draw_inputs(key, part):
    key = jax.random.fold_in(key, 11)
    full_shape = (REPLICAS, MICRO, SEQ, D)
    base_key, factor_all = rough_scales(key, full_shape, 1.1513)
    return rough_values(base_key, full_shape, factor_all).astype(jnp.bfloat16)


def draw_send_memory(key, part):
    key = jax.random.fold_in(key, 23)
    full_shape = (SECTIONS, REPLICAS, MICRO, SEQ, D)
    base_key, factor_all = rough_scales(key, full_shape, 1.1513)
    return rough_values(base_key, full_shape, factor_all).astype(jnp.bfloat16)


def draw_recv_memory(key, part):
    key = jax.random.fold_in(key, 37)
    full_shape = (SECTIONS, REPLICAS, MICRO, SEQ, D)
    base_key, factor_all = rough_scales(key, full_shape, 1.1513)
    return rough_values(base_key, full_shape, factor_all).astype(jnp.bfloat16)


def strengthened(entries, rng, source, target, blocks, factor):
    owner, partner = [(jnp.arange(entries.shape[dim]) // (entries.shape[dim] // blocks)).reshape([-1 if axis == dim else 1 for axis in range(entries.ndim)]) for dim in (source, target)]
    chosen = jax.random.permutation(rng, blocks)[partner]
    strong = (owner == chosen) | (owner == (partner + blocks // 2) % blocks)
    return jnp.where(strong, factor * entries, entries)


def block_levels(stream_key, dims, shards, low, largest):
    def one(position, shards_of):
        steps = jax.random.uniform(jax.random.fold_in(jax.random.fold_in(stream_key, 6), position), (shards_of,), jnp.float32, low / len(shards), largest / len(shards))
        return jnp.repeat(jnp.exp(steps), dims[position] // shards_of).reshape((-1,) + (1,) * (len(dims) - position - 1))

    loudness = one(*shards[0])
    for cut in shards[1:]:
        loudness = loudness * one(*cut)
    return loudness


def normal_values(key, dims, width, most, shards=(), dtype=jnp.bfloat16):
    factor_of = block_levels(key, dims, shards, -0.22, 0.18) if shards else 1.0
    array = jax.random.normal(key, dims, jnp.float32) * width * factor_of
    return jnp.minimum(jnp.maximum(array, -most), most).astype(dtype)


def bell_draw_with(stream_key, shape, scale, most, pieces, heavy, dtype=jnp.bfloat16):
    entries = scale * jax.random.normal(stream_key, shape, jnp.float32)
    if pieces:
        entries = entries * block_levels(stream_key, shape, pieces, -0.22, 0.18)
    return jnp.clip(strengthened(entries, jax.random.fold_in(stream_key, 3), *heavy), -most, most).astype(dtype)


def setup_inputs(seed: int = 0) -> dict:
    key_of = jax.random.split(jax.random.key(seed), 9)
    return {
        "inputs": draw_inputs(jax.random.fold_in(key_of[8], 71), 0),
        "cotangent": bell_draw_with(key_of[1], (REPLICAS, MICRO, SEQ, D), ((REPLICAS * MICRO * SEQ) ** -0.5), 0.09375, ((0, 32),), (0, 3, 32, 2.75)),
        "send_memory": draw_send_memory(jax.random.fold_in(key_of[8], 71), 0),
        "recv_memory": draw_recv_memory(jax.random.fold_in(key_of[8], 71), 0),
        "sample_ids": jax.vmap(lambda own: jax.random.permutation(own, MICRO))(jax.random.split(key_of[4], REPLICAS)).reshape((REPLICAS, MICRO)).astype(jnp.int32),
        "gains": jnp.clip(1.0 + 0.18 * jax.random.normal(key_of[5], (SECTIONS, LAYERS, D), jnp.float32), 0.099609375, 1.8984375).astype(jnp.bfloat16),
        "down_weight": normal_values(key_of[6], (SECTIONS, LAYERS, D, RANK), D ** -0.5, 0.0625, ((0, 8),)),
        "up_weight": normal_values(key_of[7], (SECTIONS, LAYERS, RANK, D), RANK ** -0.5, 0.75, ((0, 8),)),
    }


EPSILON = 1e-05
SQUARE_EPS = 1e-06
CLIP_RANGE = 2.0

def section_map(stream, gain_rows, down_rows, up_rows):
    for layer_no in range(down_rows.shape[0]):
        widened = stream.astype(jnp.float32)
        average = lax.optimization_barrier(jnp.mean(widened, axis=-1, keepdims=True))
        centred = widened - average
        spread = lax.optimization_barrier(jnp.mean(centred * centred, axis=-1, keepdims=True))
        normed = (centred * lax.rsqrt(spread + EPSILON) * gain_rows[layer_no].astype(jnp.float32)).astype(jnp.bfloat16)
        hidden = jax.nn.gelu(jnp.dot(normed, down_rows[layer_no], preferred_element_type=jnp.float32), approximate=True).astype(jnp.bfloat16)
        branch = jnp.dot(hidden, up_rows[layer_no], preferred_element_type=jnp.float32)
        stream = (widened + branch).astype(jnp.bfloat16)
    return stream

def block_scale(values):
    blocked = values.reshape(values.shape[:-1] + (values.shape[-1] // 128, 128))
    factor = (CLIP_RANGE * jnp.sqrt(lax.optimization_barrier(jnp.mean(blocked * blocked, axis=-1)) + SQUARE_EPS)).astype(jnp.bfloat16)
    factor = lax.optimization_barrier(factor)
    symbols = jnp.clip(blocked / factor.astype(jnp.float32)[..., None], -1.0, 1.0).astype(jnp.bfloat16)
    symbols, factor = lax.optimization_barrier((symbols.reshape(values.shape), factor))
    return (symbols, factor)

def block_value(symbols, factor):
    blocked = symbols.astype(jnp.float32).reshape(factor.shape + (128,))
    return (blocked * factor.astype(jnp.float32)[..., None]).reshape(symbols.shape)

def pull_section(stream, gain_rows, down_rows, up_rows, incoming):
    result_now, pullback = jax.vjp(section_map, stream, gain_rows, down_rows, up_rows)
    return pullback(incoming)

def reference(inputs, cotangent, send_memory, recv_memory, sample_ids, gains, down_weight, up_weight):
    sections = gains.shape[0]
    pick_rows = jax.vmap(lambda memory_rows, slot_list: memory_rows[slot_list])
    stream = inputs
    stash_list = []
    for section_no in range(sections):
        stash_list.append(stream)
        output = section_map(stream, gains[section_no], down_weight[section_no], up_weight[section_no])
        if section_no + 1 < sections:
            sent_base = pick_rows(send_memory[section_no], sample_ids)
            kept_base = pick_rows(recv_memory[section_no + 1], sample_ids)
            symbols, factor = block_scale(output.astype(jnp.float32) - sent_base.astype(jnp.float32))
            stream = (kept_base.astype(jnp.float32) + block_value(symbols, factor)).astype(jnp.bfloat16)
    incoming = cotangent
    downs = [None] * sections
    ups = [None] * sections
    gain_grads = [None] * sections
    for section_no in reversed(range(sections)):
        saved = stash_list[section_no]
        flat_in = saved.reshape((-1,) + saved.shape[2:])
        flat_cot = incoming.reshape((-1,) + incoming.shape[2:])
        gain_rows = gains[section_no]
        down_rows = down_weight[section_no]
        up_rows = up_weight[section_no]

        def accumulate(running, pair_now, gain_rows=gain_rows, down_rows=down_rows, up_rows=up_rows):
            back_grad, grad_g, grad_d, grad_u = pull_section(pair_now[0], gain_rows, down_rows, up_rows, pair_now[1])
            running = (running[0] + grad_d.astype(jnp.float32), running[1] + grad_u.astype(jnp.float32), running[2] + grad_g.astype(jnp.float32))
            return (running, back_grad)
        start_sums = (jnp.zeros(down_rows.shape, jnp.float32), jnp.zeros(up_rows.shape, jnp.float32), jnp.zeros(gain_rows.shape, jnp.float32))
        sums_now, back_all = lax.scan(accumulate, start_sums, (flat_in, flat_cot))
        downs[section_no] = sums_now[0].astype(jnp.bfloat16)
        ups[section_no] = sums_now[1].astype(jnp.bfloat16)
        gain_grads[section_no] = sums_now[2].astype(jnp.bfloat16)
        if section_no > 0:
            back_grad = back_all.reshape(incoming.shape)
            symbols, factor = block_scale(back_grad.astype(jnp.float32))
            incoming = block_value(symbols, factor).astype(jnp.bfloat16)
    return (jnp.stack(downs), jnp.stack(ups), jnp.stack(gain_grads))
```

```python
import functools
import math

import jax
import jax.numpy as jnp
from jax import lax
from jax.experimental import pallas as pl
from jax.experimental.pallas import tpu as pltpu
from jax.sharding import PartitionSpec as P

MESH = pl.DeviceIdType.MESH
F32 = jnp.float32
BF16 = jnp.bfloat16
EPSILON = 1e-05
SQUARE_EPS = 1e-06
D = 7168
RANK = 64
SHARD = 1792
BLOCKS = 14
TOKENS = 64
SECTIONS = 8
SUB = 224
AHEAD = 8
ROOT = math.sqrt(2.0 / math.pi)
CUBE = 0.044715


def dot_nn(a, b):
    return lax.dot_general(a, b, (((1,), (0,)), ((), ())), preferred_element_type=F32)


def dot_nt(a, b):
    return lax.dot_general(a, b, (((1,), (1,)), ((), ())), preferred_element_type=F32)


def dot_tn(a, b):
    return lax.dot_general(a, b, (((0,), (0,)), ((), ())), preferred_element_type=F32)


def scaled_value(v):
    square = jnp.mean(v * v, axis=-1, keepdims=True)
    factor = (2.0 * jnp.sqrt(square + SQUARE_EPS)).astype(BF16).astype(F32)
    symbols = jnp.clip(v * (1.0 / factor), -1.0, 1.0).astype(BF16).astype(F32)
    return symbols * factor


def kernel(
    ids, inp, cot, snd, rcv, dwt, upw, aux, out_d, out_u,
    w, ms, mr, ax, xs, xg, nx, dy, inv, cov, msg, pre_s, hid_s, stat, dpre_s, gp_s,
    g, cr, hs, xr, ks, zr, fs, orr,
    loc_sem, own_send, w1_recv, ax_recv, ms_recv, mr_recv, w2_send, w2_recv, w3_send, w3_recv,
    msg_send, msg_recv, r0_send, r0_recv, r1_send, r1_recv, r2_send, r2_recv, r3_send, r3_recv,
):
    sec = lax.axis_index("section")
    rep = lax.axis_index("dp")
    y = sec // 2
    zh = sec % 2
    zl = rep // 8
    xx = (rep // 2) % 4
    co = rep % 2
    z = zh * 4 + zl
    w_layer = xx // 2
    w_kind = xx % 2
    half = pl.ds(pl.multiple_of(co * 32, 32), 32)
    other_half = pl.ds(pl.multiple_of((1 - co) * 32, 32), 32)
    sibling = {"dp": rep + 1 - 2 * co}
    home_x = z // 2
    home_core = z % 2

    def columns(at):
        return pl.ds(pl.multiple_of(at * SHARD, 128), SHARD)

    def remote(src, dst, send, recv, where):
        return pltpu.make_async_remote_copy(
            src_ref=src, dst_ref=dst, send_sem=send, recv_sem=recv, device_id=where, device_id_type=MESH
        )

    def x_peer(d):
        return {"dp": zl * 8 + ((xx + d) % 4) * 2 + co}

    def z_peer(d):
        other = (z + d) % 8
        return {"section": y * 2 + other // 4, "dp": (other % 4) * 8 + xx * 2 + co}

    def home(t):
        return {"section": t, "dp": y * 8 + home_x * 2 + home_core}

    def is_home(t):
        return jnp.logical_and(t == sec, y * 8 + home_x * 2 + home_core == rep)

    mine = columns(y)
    local = [
        pltpu.make_async_copy(inp.at[0, :, :, mine], inv, loc_sem.at[0]),
        pltpu.make_async_copy(cot.at[0, :, :, mine], cov, loc_sem.at[1]),
        pltpu.make_async_copy(dwt.at[0, :, :, mine], w.at[sec, :, 0], loc_sem.at[2]),
        pltpu.make_async_copy(upw.at[0, :, :, mine], w.at[sec, :, 1], loc_sem.at[3]),
        pltpu.make_async_copy(aux.at[y], ax.at[sec], loc_sem.at[4]),
        pltpu.make_async_copy(snd.at[0, 0, pl.ds(zh * 4, 4), :, mine], ms.at[sec], loc_sem.at[5]),
        pltpu.make_async_copy(rcv.at[0, 0, pl.ds(zh * 4, 4), :, mine], mr.at[sec], loc_sem.at[6]),
    ]
    for copy in local:
        copy.start()

    barrier = pltpu.get_barrier_semaphore()

    def tell(where):
        pl.semaphore_signal(barrier, inc=1, device_id=where, device_id_type=MESH)

    for d in range(1, 8):
        tell({"section": (sec + d) % 8})
        tell(z_peer(d))
    for d in range(1, 4):
        tell(x_peer(d))
    tell(sibling)
    source_z = xx * 2 + co
    for q in range(8):
        source_section = zl * 2 + source_z // 4
        source_rep = (source_z % 4) * 8 + q
        here = jnp.logical_and(source_section == sec, source_rep == rep)

        @pl.when(jnp.logical_not(here))
        def _():
            tell({"section": source_section, "dp": source_rep})

    home_is_mine = y * 8 + home_x * 2 + home_core == rep
    pl.semaphore_wait(barrier, 7 + 7 + 3 + 1 + 8 - home_is_mine.astype(jnp.int32))

    def own_copies(d, kind):
        t2 = (sec + d) % 8
        there = columns(t2 // 2)
        slots = pl.ds((t2 % 2) * 4, 4)
        where = {"section": t2}
        if kind == 0:
            return remote(
                dwt.at[0, w_layer, half, there], w.at[sec, w_layer, 0, half], own_send.at[d - 1, 0], w1_recv.at[sec], where
            )
        if kind == 1:
            return remote(
                upw.at[0, w_layer, half, there], w.at[sec, w_layer, 1, half], own_send.at[d - 1, 0], w1_recv.at[sec], where
            )
        if kind == 2:
            return remote(aux.at[t2 // 2], ax.at[sec], own_send.at[d - 1, 1], ax_recv.at[sec], where)
        if kind == 3:
            return remote(snd.at[0, 0, slots, :, there], ms.at[sec], own_send.at[d - 1, 2], ms_recv.at[sec], where)
        return remote(rcv.at[0, 0, slots, :, there], mr.at[sec], own_send.at[d - 1, 3], mr_recv.at[sec], where)

    def each_target(action):
        def weights(d, unused):
            @pl.when(w_kind == 0)
            def _():
                action(own_copies(d, 0))

            @pl.when(w_kind == 1)
            def _():
                action(own_copies(d, 1))

            action(own_copies(d, 2))
            return unused

        def received(d, unused):
            action(own_copies(d, 4))
            return unused

        def sent(d, unused):
            action(own_copies(d, 3))
            return unused

        lax.fori_loop(1, 8, weights, 0)

        @pl.when(sec > 0)
        def _():
            lax.fori_loop(1, 8, received, 0)

        @pl.when(sec < SECTIONS - 1)
        def _():
            lax.fori_loop(1, 8, sent, 0)

    @pl.when(sec < AHEAD)
    def _():
        each_target(lambda copy: copy.start())

    for copy in local:
        copy.wait()

    for i in range(4):
        slot = zh * 4 + i
        place = jnp.int32(0)
        for m in range(8):
            place = jnp.where(ids[0, m] == slot, m, place)
        xs[0, i * 16 : (i + 1) * 16, :] = inv[place]
        dy[i * 16 : (i + 1) * 16, :] = cov[place]

    def w_part(t, kind_x):
        return w.at[t, kind_x // 2, kind_x % 2, half]

    def w2_copy(t, d):
        return remote(w_part(t, xx), w_part(t, xx), w2_send.at[t, d - 1], w2_recv.at[t, xx], x_peer(d))

    def pass_over_x(t):
        @pl.when(t != sec)
        def _():
            remote(w_part(t, xx), w_part(t, xx), own_send.at[0, 0], w1_recv.at[t], sibling).wait_recv()
            for d in range(1, 4):
                w2_copy(t, d).start()

    def w3_copy(t):
        return remote(w.at[t, :, :, half], w.at[t, :, :, half], w3_send.at[t], w3_recv.at[t], sibling)

    def w3_arrival(t):
        return remote(w.at[t, :, :, other_half], w.at[t, :, :, other_half], w3_send.at[t], w3_recv.at[t], sibling)

    def pass_to_core(t):
        @pl.when(t != sec)
        def _():
            for d in range(1, 4):
                source = (xx + d) % 4
                remote(w_part(t, source), w_part(t, source), w2_send.at[t, 0], w2_recv.at[t, source], sibling).wait_recv()
            w3_copy(t).start()

    def exchange_copy(par, d):
        return remote(
            msg.at[par, y], msg.at[par, y], msg_send.at[par, d - 1], msg_recv.at[par, y],
            {"section": ((y + d) % 4) * 2 + zh},
        )

    def exchange_start(par, value):
        msg[par, y] = value
        for d in (2, 1, 3):
            exchange_copy(par, d).start()

    def exchange_sent(par):
        for d in range(1, 4):
            exchange_copy(par, d).wait_send()

    def exchange_wait(par):
        for d in range(1, 4):
            source = (y + d) % 4
            remote(
                msg.at[par, source], msg.at[par, source], msg_send.at[par, d - 1], msg_recv.at[par, source], sibling
            ).wait_recv()

    def gain_blocks(t, l, first, count):
        rows = [ax[t, l * BLOCKS + b : l * BLOCKS + b + 1, :] for b in range(first, first + count)]
        return jnp.concatenate(rows, axis=-1) if count > 1 else rows[0]

    def gain_products(t, l):
        out = []
        for j in range(4):
            row = 28 + 2 * l + j // 2
            out.append(ax[t, row : row + 1, (j % 2) * 64 : (j % 2) * 64 + 64])
        return out

    def both(t, l):
        return w[t, l].reshape(2 * RANK, SHARD)

    pass_over_x(0)
    pass_over_x(1)
    pass_to_core(0)

    def forward(t, carry):
        @pl.when(t + AHEAD == sec)
        def _():
            each_target(lambda copy: copy.start())

        @pl.when(t != sec)
        def _():
            w3_arrival(t).wait_recv()
            remote(ax.at[t], ax.at[t], own_send.at[0, 1], ax_recv.at[t], sibling).wait_recv()

        for l in range(2):
            at = 2 * t + l
            gain = gain_blocks(t, l, 0, BLOCKS)
            centres, spreads = [], []
            for i in range(4):
                rows = slice(i * 16, (i + 1) * 16)
                xv = xs[at, rows, :].astype(F32)
                centre = jnp.sum(xv, axis=-1, keepdims=True) * (1.0 / SHARD)
                moved = xv - centre
                spreads.append(jnp.sum(moved * moved, axis=-1, keepdims=True))
                centres.append(centre)
                xg[rows, :] = (moved * gain).astype(BF16)
            centre = jnp.concatenate(centres, axis=0)
            spread = jnp.concatenate(spreads, axis=0)
            part = dot_nt(xg[...], both(t, l))
            lane = lax.broadcasted_iota(jnp.int32, (TOKENS, 128), 1)
            packed = part
            for first, number in ((64, centre), (67, spread)):
                rest = number
                for step in range(3):
                    piece = rest.astype(BF16).astype(F32)
                    packed = jnp.where(lane == first + step, piece, packed)
                    rest = rest - piece

            @pl.when(t > 0)
            def _(l=l):
                exchange_sent(l)

            exchange_start(l, packed.astype(BF16))

            if l == 0:
                @pl.when(t < SECTIONS - 2)
                def _():
                    pass_over_x(t + 2)
            else:
                @pl.when(t < SECTIONS - 1)
                def _():
                    pass_to_core(t + 1)

            exchange_wait(l)
            total = jnp.zeros((TOKENS, 128), F32)
            means = []
            spread = jnp.zeros((TOKENS, 1), F32)
            for j in range(4):
                got = msg[l, j].astype(F32)
                total = total + got
                means.append(got[:, 64:65] + got[:, 65:66] + got[:, 66:67])
                spread = spread + (got[:, 67:68] + got[:, 68:69] + got[:, 69:70])
            mean = 0.25 * (means[0] + means[1] + means[2] + means[3])
            products = gain_products(t, l)
            pre = total[:, :RANK]
            for j in range(4):
                apart = means[j] - mean
                spread = spread + SHARD * (apart * apart)
                pre = pre + apart * products[j]
            rstd = lax.rsqrt(spread * (1.0 / D) + EPSILON)
            pre = pre * rstd
            hidden = (0.5 * pre * (1.0 + jnp.tanh(ROOT * (pre + CUBE * pre * pre * pre)))).astype(BF16)
            pre_s[at] = pre
            hid_s[at] = hidden
            stat[at, 0] = jnp.broadcast_to(mean, (TOKENS, 128))
            stat[at, 1] = jnp.broadcast_to(rstd, (TOKENS, 128))

            if l == 0:
                for n in range(7):
                    cols = slice(n * 256, (n + 1) * 256)
                    branch = dot_nn(hidden, w[t, l, 1, :, cols])
                    xs[at + 1, :, cols] = (xs[at, :, cols].astype(F32) + branch).astype(BF16)
            else:
                @pl.when(t < SECTIONS - 1)
                def _(hidden=hidden, at=at):
                    @pl.when(t != sec)
                    def _():
                        remote(ms.at[t], ms.at[t], own_send.at[0, 2], ms_recv.at[t], sibling).wait_recv()

                    @pl.when(t + 1 != sec)
                    def _():
                        remote(mr.at[t + 1], mr.at[t + 1], own_send.at[0, 3], mr_recv.at[t + 1], sibling).wait_recv()

                    for n in range(7):
                        branch = dot_nn(hidden, w[t, 1, 1, :, n * 256 : (n + 1) * 256])
                        for b in range(2):
                            cols = slice(n * 256 + b * 128, n * 256 + b * 128 + 128)
                            out = (xs[at, :, cols].astype(F32) + branch[:, b * 128 : b * 128 + 128]).astype(BF16)
                            old = ms[t, :, :, cols].reshape(TOKENS, 128).astype(F32)
                            kept = mr[t + 1, :, :, cols].reshape(TOKENS, 128).astype(F32)
                            value = scaled_value(out.astype(F32) - old)
                            xs[at + 1, :, cols] = (kept + value).astype(BF16)
        return carry

    lax.fori_loop(0, SECTIONS, forward, 0)

    def begin(t, l):
        at = 2 * t + l
        par = 1 - l
        part = dot_nt(dy[...], both(t, l))
        exchange_sent(par)
        exchange_start(par, part.astype(BF16))
        pre = pre_s[at]
        tanh = jnp.tanh(ROOT * (pre + CUBE * pre * pre * pre))
        slope = 0.5 * (1.0 + tanh) + 0.5 * pre * (1.0 - tanh * tanh) * ROOT * (1.0 + 3.0 * CUBE * pre * pre)
        gp_s[...] = slope
        mean = stat[at, 0]
        rstd = stat[at, 1]
        for b in range(BLOCKS):
            cols = slice(b * 128, (b + 1) * 128)
            normed = (xs[at, :, cols].astype(F32) - mean) * rstd * gain_blocks(t, l, b, 1)
            nx[l, :, cols] = normed.astype(BF16)
        hidden = hid_s[at]
        for n in range(7):
            cols = slice(n * 256, (n + 1) * 256)
            g[t, l, 1, :, cols] = dot_tn(hidden, dy[:, cols]).astype(BF16)

    def down_gradient(t, l):
        late = dpre_s[l]
        for n in range(7):
            cols = slice(n * 256, (n + 1) * 256)
            g[t, l, 0, :, cols] = dot_tn(late, nx[l, :, cols]).astype(BF16)

    def finish(t, l):
        at = 2 * t + l
        par = 1 - l
        exchange_wait(par)
        total = jnp.zeros((TOKENS, 128), F32)
        for j in range(4):
            total = total + msg[par, j].astype(F32)
        late = (total[:, RANK:].astype(BF16).astype(F32) * gp_s[...]).astype(BF16)
        dpre_s[l] = late
        wide = late.astype(F32)

        def through():
            products = gain_products(t, l)
            across = products[0] + products[1] + products[2] + products[3]
            first = jnp.sum(wide * across, axis=-1, keepdims=True) * (1.0 / D)
            second = jnp.sum(wide * pre_s[at], axis=-1, keepdims=True) * (1.0 / D)
            mean = stat[at, 0]
            rstd = stat[at, 1]
            for n in range(7):
                moved = dot_nn(late, w[t, l, 0, :, n * 256 : (n + 1) * 256])
                for b in range(2):
                    cols = slice(n * 256 + b * 128, n * 256 + b * 128 + 128)
                    dn = moved[:, b * 128 : b * 128 + 128].astype(BF16).astype(F32)
                    hat = (xs[at, :, cols].astype(F32) - mean) * rstd
                    back = rstd * (dn * gain_blocks(t, l, 2 * n + b, 1) - first - hat * second)
                    back = (dy[:, cols].astype(F32) + back).astype(BF16)
                    if l == 0:
                        back = scaled_value(back.astype(F32)).astype(BF16)
                    dy[:, cols] = back

        if l == 0:
            pl.when(t > 0)(through)
        else:
            through()

    def r0_copy(t):
        return remote(g.at[t, :, :, other_half], cr.at[t], r0_send.at[t], r0_recv.at[t], sibling)

    def r1_copy(t, d):
        there = (xx + d) % 4
        return remote(
            hs.at[t, there // 2, there % 2], xr.at[t, 3 - d], r1_send.at[t, d - 1], r1_recv.at[t, 3 - d], x_peer(d)
        )

    def r1_start(t):
        r0_copy(t).wait_recv()
        for l in range(2):
            for kind in range(2):
                hs[t, l, kind] = (g[t, l, kind, half, :].astype(F32) + cr[t, l, kind].astype(F32)).astype(BF16)
        for d in range(1, 4):
            r1_copy(t, d).start()

    def r2_copy(t, d):
        there = (z + d) % 8
        return remote(
            ks.at[t, there], zr.at[t, 7 - d], r2_send.at[t, d - 1], r2_recv.at[t, 7 - d], z_peer(d)
        )

    def r2_start(t):
        for d in range(1, 4):
            remote(xr.at[t, d - 1], xr.at[t, d - 1], r1_send.at[t, 0], r1_recv.at[t, d - 1], sibling).wait_recv()
        for k in range(8):
            begin_at = k * SUB // 128 * 128
            shift = k * SUB - begin_at
            width = -(-(shift + SUB) // 128) * 128
            cols = slice(begin_at, begin_at + width)
            total = hs[t, w_layer, w_kind, :, cols].astype(F32)
            for d in range(3):
                total = total + xr[t, d, :, cols].astype(F32)
            if shift:
                total = pltpu.roll(total, width - shift, 1)
            ks[t, k] = total[:, :256].astype(BF16)
        for d in range(1, 8):
            r2_copy(t, d).start()

    def r3_copy(t):
        return remote(fs.at[t], orr.at[rep % 8], r3_send.at[t], r3_recv.at[rep % 8], home(t))

    def r3_start(t):
        total = ks[t, z].astype(F32)
        for d in range(7):
            remote(zr.at[t, d], zr.at[t, d], r2_send.at[t, 0], r2_recv.at[t, d], sibling).wait_recv()
            total = total + zr[t, d].astype(F32)
        fs[t] = total.astype(BF16)

        @pl.when(is_home(t))
        def _():
            orr[rep % 8] = fs[t]

        @pl.when(jnp.logical_not(is_home(t)))
        def _():
            r3_copy(t).start()

    def backward(k, carry):
        t = SECTIONS - 1 - k
        here = k < SECTIONS
        after = jnp.logical_and(k >= 1, k < SECTIONS + 1)
        later = k >= 2

        @pl.when(here)
        def _():
            begin(t, 1)

        @pl.when(after)
        def _():
            down_gradient(t + 1, 0)
            r0_copy(t + 1).start()

        @pl.when(later)
        def _():
            r2_start(t + 2)

        @pl.when(here)
        def _():
            finish(t, 1)
            begin(t, 0)
            down_gradient(t, 1)

        @pl.when(after)
        def _():
            r1_start(t + 1)

        @pl.when(later)
        def _():
            r3_start(t + 2)

        @pl.when(here)
        def _():
            finish(t, 0)

        return carry

    lax.fori_loop(0, SECTIONS + 2, backward, 0)

    for q in range(8):
        source_rep = (source_z % 4) * 8 + q
        here = jnp.logical_and(zl * 2 + source_z // 4 == sec, source_rep == rep)

        @pl.when(jnp.logical_not(here))
        def _(q=q):
            remote(orr.at[q], orr.at[q], r3_send.at[0], r3_recv.at[q], sibling).wait_recv()

    for l in range(2):
        for part in range(2):
            rows = slice(part * 32, (part + 1) * 32)
            out_d[l, rows, :] = orr[l * 4 + part][:, :SUB]
            out_u[l, rows, :] = orr[l * 4 + 2 + part][:, :SUB]

    each_target(lambda copy: copy.wait_send())
    exchange_sent(0)
    exchange_sent(1)

    def drain(t, carry):
        @pl.when(t != sec)
        def _():
            for d in range(1, 4):
                w2_copy(t, d).wait_send()
            w3_copy(t).wait_send()

        r0_copy(t).wait_send()
        for d in range(1, 4):
            r1_copy(t, d).wait_send()
        for d in range(1, 8):
            r2_copy(t, d).wait_send()

        @pl.when(jnp.logical_not(is_home(t)))
        def _():
            r3_copy(t).wait_send()

        return carry

    lax.fori_loop(0, SECTIONS, drain, 0)


def local(inputs, cotangent, send_memory, recv_memory, sample_ids, gains, down_weight, up_weight):
    dwt = jnp.swapaxes(down_weight, 2, 3)
    gain = gains[0].astype(F32)
    products = (gain[:, None, :] * dwt[0].astype(F32)).reshape(2, RANK, 4, SHARD).sum(-1)
    products = jnp.swapaxes(products, 1, 2).reshape(4, 128)
    rows = jnp.swapaxes(gain.reshape(2, 4, BLOCKS, 128), 0, 1).reshape(4, 2 * BLOCKS, 128)
    aux = jnp.concatenate([rows, jnp.broadcast_to(products, (4, 4, 128))], axis=1)

    anywhere = pl.BlockSpec(memory_space=pl.ANY)
    vmem = pl.BlockSpec(memory_space=pltpu.VMEM)
    sem = pltpu.SemaphoreType.DMA
    grad_down, grad_up = pl.pallas_call(
        kernel,
        out_shape=(
            jax.ShapeDtypeStruct((2, RANK, SUB), BF16),
            jax.ShapeDtypeStruct((2, RANK, SUB), BF16),
        ),
        in_specs=[pl.BlockSpec(memory_space=pltpu.SMEM)] + [anywhere] * 7,
        out_specs=(vmem, vmem),
        scratch_shapes=[
            pltpu.VMEM((8, 2, 2, RANK, SHARD), BF16),
            pltpu.VMEM((8, 4, 16, SHARD), BF16),
            pltpu.VMEM((8, 4, 16, SHARD), BF16),
            pltpu.VMEM((8, 32, 128), F32),
            pltpu.VMEM((16, TOKENS, SHARD), BF16),
            pltpu.VMEM((TOKENS, SHARD), BF16),
            pltpu.VMEM((2, TOKENS, SHARD), BF16),
            pltpu.VMEM((TOKENS, SHARD), BF16),
            pltpu.VMEM((8, 16, SHARD), BF16),
            pltpu.VMEM((8, 16, SHARD), BF16),
            pltpu.VMEM((2, 4, TOKENS, 128), BF16),
            pltpu.VMEM((16, TOKENS, RANK), F32),
            pltpu.VMEM((16, TOKENS, RANK), BF16),
            pltpu.VMEM((16, 2, TOKENS, 128), F32),
            pltpu.VMEM((2, TOKENS, RANK), BF16),
            pltpu.VMEM((TOKENS, RANK), F32),
            pltpu.VMEM((8, 2, 2, RANK, SHARD), BF16),
            pltpu.VMEM((8, 2, 2, 32, SHARD), BF16),
            pltpu.VMEM((8, 2, 2, 32, SHARD), BF16),
            pltpu.VMEM((8, 3, 32, SHARD), BF16),
            pltpu.VMEM((8, 8, 32, 256), BF16),
            pltpu.VMEM((8, 7, 32, 256), BF16),
            pltpu.VMEM((8, 32, 256), BF16),
            pltpu.VMEM((8, 32, 256), BF16),
            sem((7,)),
            sem((7, 4)),
            sem((8,)),
            sem((8,)),
            sem((8,)),
            sem((8,)),
            sem((8, 3)),
            sem((8, 4)),
            sem((8,)),
            sem((8,)),
            sem((2, 3)),
            sem((2, 4)),
            sem((8,)),
            sem((8,)),
            sem((8, 3)),
            sem((8, 3)),
            sem((8, 7)),
            sem((8, 7)),
            sem((8,)),
            sem((8,)),
        ],
        compiler_params=pltpu.CompilerParams(
            collective_id=0, has_side_effects=True, vmem_limit_bytes=56 * 1024 * 1024
        ),
        name="relay",
    )(sample_ids, inputs, cotangent, send_memory, recv_memory, dwt, up_weight, aux)

    start = lax.axis_index("dp") * SUB
    own_down = lax.dynamic_slice_in_dim(dwt[0], start, SUB, 2).astype(F32)
    own_gain = lax.dynamic_slice_in_dim(gain, start, SUB, 1)
    grad_gain = jnp.sum(own_down * grad_down.astype(F32), axis=1) / own_gain
    return (
        jnp.swapaxes(grad_down, 1, 2)[None],
        grad_up[None],
        grad_gain.astype(BF16)[None],
    )


def solution(mesh):
    in_specs = (
        P("dp", None, None, None),
        P("dp", None, None, None),
        P("section", "dp", None, None, None),
        P("section", "dp", None, None, None),
        P("dp", None),
        P("section", None, None),
        P("section", None, None, None),
        P("section", None, None, None),
    )
    out_specs = (
        P("section", None, "dp", None),
        P("section", None, None, "dp"),
        P("section", None, "dp"),
    )
    return jax.shard_map(local, mesh=mesh, in_specs=in_specs, out_specs=out_specs, check_vma=False)
```

```python
import functools
import math

import jax
import jax.numpy as jnp
from jax import lax
from jax.experimental import pallas as pl
from jax.experimental.pallas import tpu as pltpu
from jax.sharding import PartitionSpec as P

MESH = pl.DeviceIdType.MESH
F32 = jnp.float32
BF16 = jnp.bfloat16
EPSILON = 1e-05
SQUARE_EPS = 1e-06
D = 7168
RANK = 64
SHARD = 1792
BLOCKS = 14
TOKENS = 64
SECTIONS = 8
SUB = 224
ROOT = math.sqrt(2.0 / math.pi)
CUBE = 0.044715


def dot_nn(a, b):
    return lax.dot_general(a, b, (((1,), (0,)), ((), ())), preferred_element_type=F32)


def dot_nt(a, b):
    return lax.dot_general(a, b, (((1,), (1,)), ((), ())), preferred_element_type=F32)


def dot_tn(a, b):
    return lax.dot_general(a, b, (((0,), (0,)), ((), ())), preferred_element_type=F32)


def scaled_value(v):
    square = jnp.mean(v * v, axis=-1, keepdims=True)
    factor = (2.0 * jnp.sqrt(square + SQUARE_EPS)).astype(BF16).astype(F32)
    symbols = jnp.clip(v * (1.0 / factor), -1.0, 1.0).astype(BF16).astype(F32)
    return symbols * factor


def kernel(
    ids, inp, cot, snd, rcv, dwt, upw, gains, out_d, out_u,
    w, ms, mr, ax, px, pv, px_own, pv_own, all_gains, rw, xs, xg, dy, dy0, inv, cov, msg, msb,
    pre_s, hid_s, stat, far_s, dpre_s, gp_s,
    g, cr, hs, xr, ks, zr, fs, orr,
    loc_sem, own_send, ax_send, w1_recv, ax_recv, ms_recv, mr_recv, zw_send, zs_send, zr_send, w2_send, w2_recv, w3_send, w3_recv,
    msg_send, msg_recv, msb_send, msb_recv, r0_send, r0_recv, r1_send, r1_recv, r2_send, r2_recv, r3_send, r3_recv,
):
    sec = lax.axis_index("section")
    rep = lax.axis_index("dp")
    y = sec // 2
    zh = sec % 2
    zl = rep // 8
    xx = (rep // 2) % 4
    co = rep % 2
    z = zh * 4 + zl
    w_layer = xx // 2
    w_kind = xx % 2
    half = pl.ds(pl.multiple_of(co * 32, 32), 32)
    other_half = pl.ds(pl.multiple_of((1 - co) * 32, 32), 32)
    sibling = {"dp": rep + 1 - 2 * co}
    home_x = z // 2
    home_core = z % 2

    def columns(at):
        return pl.ds(pl.multiple_of(at * SHARD, 128), SHARD)

    def remote(src, dst, send, recv, where):
        return pltpu.make_async_remote_copy(
            src_ref=src, dst_ref=dst, send_sem=send, recv_sem=recv, device_id=where, device_id_type=MESH
        )

    def x_peer(d):
        return {"dp": zl * 8 + ((xx + d) % 4) * 2 + co}

    def z_peer(d):
        other = (z + d) % 8
        return {"section": y * 2 + other // 4, "dp": (other % 4) * 8 + xx * 2 + co}

    def home(t):
        return {"section": t, "dp": y * 8 + home_x * 2 + home_core}

    def is_home(t):
        return jnp.logical_and(t == sec, y * 8 + home_x * 2 + home_core == rep)

    mine = columns(y)
    local = [
        pltpu.make_async_copy(inp.at[0, :, :, mine], inv, loc_sem.at[0]),
        pltpu.make_async_copy(cot.at[0, :, :, mine], cov, loc_sem.at[1]),
        pltpu.make_async_copy(dwt.at[0, :, :, mine], w.at[sec, :, 0], loc_sem.at[2]),
        pltpu.make_async_copy(upw.at[0, :, :, mine], w.at[sec, :, 1], loc_sem.at[3]),
        pltpu.make_async_copy(gains, all_gains, loc_sem.at[4]),
        pltpu.make_async_copy(snd.at[0, 0, :, :, mine], ms.at[sec], loc_sem.at[5]),
        pltpu.make_async_copy(rcv.at[0, 0, :, :, mine], mr.at[sec], loc_sem.at[6]),
    ]
    for j in range(4):
        cols = slice(j * SHARD, (j + 1) * SHARD)
        local.append(pltpu.make_async_copy(dwt.at[0, :, :, cols], g.at[j, :, 0], loc_sem.at[7 + 2 * j]))
        local.append(pltpu.make_async_copy(upw.at[0, :, :, cols], g.at[j, :, 1], loc_sem.at[8 + 2 * j]))
    for copy in local:
        copy.start()

    barrier = pltpu.get_barrier_semaphore()

    def tell(where):
        pl.semaphore_signal(barrier, inc=1, device_id=where, device_id_type=MESH)

    for d in range(1, 8):
        tell({"section": (sec + d) % 8})
        tell(z_peer(d))
    for d in range(1, 4):
        tell(x_peer(d))
    tell(sibling)
    source_z = xx * 2 + co
    for q in range(8):
        source_section = zl * 2 + source_z // 4
        source_rep = (source_z % 4) * 8 + q
        here = jnp.logical_and(source_section == sec, source_rep == rep)

        @pl.when(jnp.logical_not(here))
        def _():
            tell({"section": source_section, "dp": source_rep})

    home_is_mine = y * 8 + home_x * 2 + home_core == rep
    pl.semaphore_wait(barrier, 7 + 7 + 3 + 1 + 8 - home_is_mine.astype(jnp.int32))

    own_slots = pl.ds(zh * 4, 4)
    far_slots = pl.ds(4 - zh * 4, 4)
    across = {"section": y * 2 + 1 - zh}

    def y_copy(d, kind):
        t2 = ((y + d) % 4) * 2 + zh
        there = columns((y + d) % 4)
        where = {"section": t2}
        if kind == 0:
            return remote(
                dwt.at[0, w_layer, half, there], w.at[sec, w_layer, 0, half], own_send.at[d - 1, 0], w1_recv.at[sec], where
            )
        if kind == 1:
            return remote(
                upw.at[0, w_layer, half, there], w.at[sec, w_layer, 1, half], own_send.at[d - 1, 0], w1_recv.at[sec], where
            )
        slots, number = (far_slots, 0) if kind in (2, 3) else (own_slots, 1)
        if kind in (2, 4):
            return remote(
                rcv.at[0, 0, slots, :, there], mr.at[sec, slots], own_send.at[d - 1, kind - 1], mr_recv.at[sec, number], where
            )
        return remote(
            snd.at[0, 0, slots, :, there], ms.at[sec, slots], own_send.at[d - 1, kind - 1], ms_recv.at[sec, number], where
        )

    def aux_copies(d):
        t2 = (sec + d) % 8
        where = {"section": t2}
        return (
            remote(all_gains.at[t2 // 2], ax.at[sec], ax_send.at[d - 1, 0], ax_recv.at[sec, 0], where),
            remote(px_own, px.at[sec], ax_send.at[d - 1, 1], ax_recv.at[sec, 1], where),
            remote(pv_own, pv.at[sec], ax_send.at[d - 1, 2], ax_recv.at[sec, 2], where),
        )

    def y_weights(action):
        def some(kind):
            for d in (1, 3, 2):
                action(y_copy(d, kind))

        pl.when(w_kind == 0)(lambda: some(0))
        pl.when(w_kind == 1)(lambda: some(1))

    def y_memories(action):
        def some(kind):
            for d in (1, 3, 2):
                action(y_copy(d, kind))

        for kind in range(2, 6):
            pl.when(sec > 0 if kind % 2 == 0 else sec < SECTIONS - 1)(functools.partial(some, kind))

    def y_aux(action):
        for d in range(1, 8):
            for copy in aux_copies(d):
                action(copy)

    y_weights(lambda copy: copy.start())
    for copy in local:
        copy.wait()

    def gain_blocks(rows_ref, l, first, count):
        rows = [rows_ref[l * BLOCKS + b : l * BLOCKS + b + 1, :] for b in range(first, first + count)]
        return jnp.concatenate(rows, axis=-1) if count > 1 else rows[0]

    def fold(weights, rows_ref, into):
        for l in range(2):
            gained = weights[l, 0].astype(F32) * gain_blocks(rows_ref, l, 0, BLOCKS)
            into[l * RANK : (l + 1) * RANK, :] = gained.astype(BF16)
        into[2 * RANK :, :] = weights[0, 1]

    ones = jnp.ones((16, SHARD), BF16)
    products = jnp.zeros((RANK, 2 * RANK), F32)
    up_sum = jnp.zeros((RANK, 16), F32)
    whole = jnp.zeros((16, 3 * RANK), F32)
    for j in range(4):
        fold(g.at[j], all_gains.at[j], rw.at[0])
        here_sums = dot_nt(ones, rw[0])
        whole = whole + here_sums
        px_own[2 * j : 2 * j + 1, :] = here_sums[:1, : 2 * RANK]
        px_own[2 * j + 1 : 2 * j + 2, :] = jnp.concatenate([here_sums[:1, 2 * RANK :], jnp.zeros((1, RANK), F32)], axis=-1)
        up = rw[0, 2 * RANK :, :]
        products = products + dot_nt(up, rw[0, RANK:, :])
        up_sum = up_sum + dot_nt(up, ones)
    products = products - up_sum[:, :1] * (whole[:1, RANK:] * (1.0 / D))
    pv_own[...] = products.astype(BF16)
    ax[sec] = all_gains[y]
    px[sec] = px_own[...]
    pv[sec] = pv_own[...]
    y_aux(lambda copy: copy.start())
    y_memories(lambda copy: copy.start())

    for i in range(4):
        slot = zh * 4 + i
        place = jnp.int32(0)
        for m in range(8):
            place = jnp.where(ids[0, m] == slot, m, place)
        xs[0, i * 16 : (i + 1) * 16, :] = inv[place]
        dy[i * 16 : (i + 1) * 16, :] = cov[place]

    def w_part(t, kind_x):
        return w.at[t, kind_x // 2, kind_x % 2, half]

    def w2_copy(t, d):
        return remote(w_part(t, xx), w_part(t, xx), w2_send.at[t, d - 1], w2_recv.at[t, xx], x_peer(d))

    def zw_copy(t):
        return remote(w_part(t, xx), w_part(t, xx), zw_send.at[t], w1_recv.at[t], across)

    def zs_copy(t):
        return remote(ms.at[t, far_slots], ms.at[t, far_slots], zs_send.at[t], ms_recv.at[t, 1], across)

    def zr_copy(t):
        return remote(mr.at[t, far_slots], mr.at[t, far_slots], zr_send.at[t], mr_recv.at[t, 1], across)

    def ms_wait(t, number):
        slots = own_slots if number else far_slots

        @pl.when(t != sec)
        def _():
            remote(ms.at[t, slots], ms.at[t, slots], zs_send.at[t], ms_recv.at[t, number], sibling).wait_recv()

    def mr_wait(t, number):
        slots = own_slots if number else far_slots

        @pl.when(t != sec)
        def _():
            remote(mr.at[t, slots], mr.at[t, slots], zr_send.at[t], mr_recv.at[t, number], sibling).wait_recv()

    def relay(b):
        @pl.when(b % 2 == zh)
        def _():
            ms_wait(b, 0)
            zs_copy(b).start()

        @pl.when(b % 2 != zh)
        def _():
            mr_wait(b + 1, 0)
            zr_copy(b + 1).start()

    def over_x(t):
        @pl.when(t != sec)
        def _():
            remote(w_part(t, xx), w_part(t, xx), own_send.at[0, 0], w1_recv.at[t], sibling).wait_recv()

        pl.when(t % 2 == zh)(lambda: zw_copy(t).start())

        @pl.when(t != sec)
        def _():
            for d in range(1, 4):
                w2_copy(t, d).start()

    def over_x_from_far(t):
        pl.when(t % 2 != zh)(lambda: over_x(t))

    def w3_copy(t):
        return remote(w.at[t, :, :, half], w.at[t, :, :, half], w3_send.at[t], w3_recv.at[t], sibling)

    def w3_arrival(t):
        return remote(w.at[t, :, :, other_half], w.at[t, :, :, other_half], w3_send.at[t], w3_recv.at[t], sibling)

    def pass_to_core(t):
        @pl.when(t != sec)
        def _():
            for d in range(1, 4):
                source = (xx + d) % 4
                remote(w_part(t, source), w_part(t, source), w2_send.at[t, 0], w2_recv.at[t, source], sibling).wait_recv()
            w3_copy(t).start()

    def exchange_copy(buffers, par, d):
        held, send, recv = buffers
        return remote(
            held.at[par, y], held.at[par, y], send.at[par, d - 1], recv.at[par, y], {"section": ((y + d) % 4) * 2 + zh}
        )

    def exchange_start(buffers, par, value):
        buffers[0][par, y] = value
        for d in (2, 1, 3):
            exchange_copy(buffers, par, d).start()

    def exchange_sent(buffers, par):
        for d in range(1, 4):
            exchange_copy(buffers, par, d).wait_send()

    def exchange_wait(buffers, par):
        held, send, recv = buffers
        for d in range(1, 4):
            source = (y + d) % 4
            remote(
                held.at[par, source], held.at[par, source], send.at[par, d - 1], recv.at[par, source], sibling
            ).wait_recv()

    ahead = (msg, msg_send, msg_recv)
    back = (msb, msb_send, msb_recv)

    def sums_of(t, j):
        return px[t, 2 * j : 2 * j + 1, :], px[t, 2 * j + 1 : 2 * j + 2, :RANK]

    def gelu(pre):
        return (0.5 * pre * (1.0 + jnp.tanh(ROOT * (pre + CUBE * pre * pre * pre)))).astype(BF16)

    def gelu_slope(pre):
        tanh = jnp.tanh(ROOT * (pre + CUBE * pre * pre * pre))
        return 0.5 * (1.0 + tanh) + 0.5 * pre * (1.0 - tanh * tanh) * ROOT * (1.0 + 3.0 * CUBE * pre * pre)

    def ready(t):
        @pl.when(t != sec)
        def _():
            w3_arrival(t).wait_recv()
            for n, held in enumerate((ax, px, pv)):
                remote(held.at[t], held.at[t], ax_send.at[0, n], ax_recv.at[t, n], sibling).wait_recv()

        fold(w.at[t], ax.at[t], rw.at[t % 2])

    def first(i, carry):
        over_x(2 * i + zh)
        pl.when(i > 0)(lambda: relay(2 * i - 1))
        relay(2 * i)
        return carry

    lax.fori_loop(0, 4, first, 0)
    over_x_from_far(0)
    over_x_from_far(1)
    over_x_from_far(2)
    pass_to_core(0)
    pass_to_core(1)
    ready(0)

    def wide(column):
        return jnp.broadcast_to(column, (TOKENS, 128))

    def forward(t, carry):
        at = 2 * t
        par = t % 2
        centres, spreads = [], []
        for i in range(4):
            rows = slice(i * 16, (i + 1) * 16)
            xv = xs[at, rows, :].astype(F32)
            centre = jnp.sum(xv, axis=-1, keepdims=True) * (1.0 / SHARD)
            moved = xv - centre
            spreads.append(jnp.sum(moved * moved, axis=-1, keepdims=True))
            centres.append(centre)
            xg[rows, :] = moved.astype(BF16)
        centre = jnp.concatenate(centres, axis=0)
        spread = jnp.concatenate(spreads, axis=0)
        part = dot_nt(xg[...], rw[par])
        lane = lax.broadcasted_iota(jnp.int32, (TOKENS, RANK), 1)
        packed = jnp.zeros((TOKENS, RANK), F32)
        for start, number in ((0, centre), (3, spread)):
            rest = number
            for step in range(3):
                piece = rest.astype(BF16).astype(F32)
                packed = jnp.where(lane == start + step, piece, packed)
                rest = rest - piece

        pl.when(t > 1)(lambda: exchange_sent(ahead, par))
        exchange_start(ahead, par, jnp.concatenate([part, packed], axis=-1).astype(BF16))

        pl.when(t < SECTIONS - 3)(lambda: over_x_from_far(t + 3))
        pl.when(t < SECTIONS - 2)(lambda: pass_to_core(t + 2))
        pl.when(t < SECTIONS - 1)(lambda: ready(t + 1))

        exchange_wait(ahead, par)
        first = jnp.zeros((TOKENS, 2 * RANK), F32)
        second = jnp.zeros((TOKENS, 2 * RANK), F32)
        means = []
        spread = jnp.zeros((TOKENS, 1), F32)
        for j in range(4):
            first = first + msg[par, j, :, : 2 * RANK].astype(F32)
            got = msg[par, j, :, 2 * RANK :].astype(F32)
            second = second + got
            means.append(got[:, 64:65] + got[:, 65:66] + got[:, 66:67])
            spread = spread + (got[:, 67:68] + got[:, 68:69] + got[:, 69:70])
        mean = 0.25 * (means[0] + means[1] + means[2] + means[3])
        second = second[:, :RANK]
        up_mean = jnp.zeros((1, RANK), F32)
        for j in range(4):
            apart = means[j] - mean
            spread = spread + SHARD * (apart * apart)
            sums, up_sums = sums_of(t, j)
            first = first + apart * sums
            second = second + apart * up_sums
            up_mean = up_mean + up_sums * (1.0 / D)
        rstd = lax.rsqrt(spread * (1.0 / D) + EPSILON)
        pre = first[:, :RANK] * rstd
        hidden = gelu(pre)
        moved = dot_nn(hidden, pv[t])
        hidden_wide = hidden.astype(F32)
        far = second + moved[:, RANK:]
        spread1 = jnp.maximum(spread + jnp.sum(hidden_wide * (second + far), axis=-1, keepdims=True), 0.0)
        rstd1 = lax.rsqrt(spread1 * (1.0 / D) + EPSILON)
        mean1 = mean + jnp.sum(hidden_wide * up_mean, axis=-1, keepdims=True)
        pre1 = (first[:, RANK:] + moved[:, :RANK]) * rstd1
        hidden1 = gelu(pre1)
        pre_s[at] = pre
        pre_s[at + 1] = pre1
        hid_s[at] = hidden
        hid_s[at + 1] = hidden1
        far_s[t] = far
        stat[at, 0] = wide(mean)
        stat[at, 1] = wide(rstd)
        stat[at + 1, 0] = wide(mean1)
        stat[at + 1, 1] = wide(rstd1)

        def next_layer(n):
            cols = slice(n * 256, (n + 1) * 256)
            branch = dot_nn(hidden, w[t, 0, 1, :, cols])
            middle = (xs[at, :, cols].astype(F32) + branch).astype(BF16)
            xs[at + 1, :, cols] = middle
            return middle

        @pl.when(t == SECTIONS - 1)
        def _():
            for n in range(7):
                next_layer(n)

        @pl.when(t < SECTIONS - 1)
        def _():
            ms_wait(t, 1)
            mr_wait(t + 1, 1)
            for n in range(7):
                middle = next_layer(n).astype(F32)
                branch = dot_nn(hidden1, w[t, 1, 1, :, n * 256 : (n + 1) * 256])
                out = (middle + branch).astype(BF16).astype(F32)
                for b in range(2):
                    cols = slice(n * 256 + b * 128, n * 256 + b * 128 + 128)
                    old = ms[t, own_slots, :, cols].reshape(TOKENS, 128).astype(F32)
                    kept = mr[t + 1, own_slots, :, cols].reshape(TOKENS, 128).astype(F32)
                    value = scaled_value(out[:, b * 128 : b * 128 + 128] - old)
                    xs[at + 2, :, cols] = (kept + value).astype(BF16)

        return carry

    lax.fori_loop(0, SECTIONS, forward, 0)
    exchange_sent(ahead, 0)
    exchange_sent(ahead, 1)

    def begin(t, par):
        part = dot_nt(dy[...], w[t, :, 1].reshape(2 * RANK, SHARD))
        pl.when(t < SECTIONS - 2)(lambda: exchange_sent(back, par))
        exchange_start(back, par, part.astype(BF16))
        gp_s[0] = gelu_slope(pre_s[2 * t])
        gp_s[1] = gelu_slope(pre_s[2 * t + 1])
        hidden = hid_s[2 * t + 1]
        for n in range(7):
            cols = slice(n * 256, (n + 1) * 256)
            g[t, 1, 1, :, cols] = dot_tn(hidden, dy[:, cols]).astype(BF16)

    def gradients(t):
        hidden = hid_s[2 * t]
        for n in range(7):
            cols = slice(n * 256, (n + 1) * 256)
            for l in range(2):
                at = 2 * t + l
                pieces = []
                for b in (2 * n, 2 * n + 1):
                    part = xs[at, :, b * 128 : (b + 1) * 128].astype(F32)
                    pieces.append((part - stat[at, 0]) * stat[at, 1] * gain_blocks(ax.at[t], l, b, 1))
                normed = jnp.concatenate(pieces, axis=-1).astype(BF16)
                g[t, l, 0, :, cols] = dot_tn(dpre_s[l], normed).astype(BF16)
            g[t, 0, 1, :, cols] = dot_tn(hidden, dy0[:, cols]).astype(BF16)

    def finish(t, par):
        exchange_wait(back, par)
        total = jnp.zeros((TOKENS, 2 * RANK), F32)
        for j in range(4):
            total = total + msb[par, j].astype(F32)
        both_sums = px[t, 0:1, :] + px[t, 2:3, :] + px[t, 4:5, :] + px[t, 6:7, :]

        def row_means(late, l):
            numbers = late.astype(F32)
            one = jnp.sum(numbers * both_sums[:, l * RANK : (l + 1) * RANK], axis=-1, keepdims=True) * (1.0 / D)
            two = jnp.sum(numbers * pre_s[2 * t + l], axis=-1, keepdims=True) * (1.0 / D)
            return one, two

        late1 = (total[:, RANK:].astype(BF16).astype(F32) * gp_s[1]).astype(BF16)
        dpre_s[1] = late1
        one1, two1 = row_means(late1, 1)
        mean1, rstd1 = stat[2 * t + 1, 0], stat[2 * t + 1, 1]
        column = rstd1[:, :RANK]
        inner = total[:, :RANK] + column * (dot_nt(late1, pv[t, :, :RANK]) - two1 * column * far_s[t])
        late0 = (inner.astype(BF16).astype(F32) * gp_s[0]).astype(BF16)
        dpre_s[0] = late0
        for n in range(7):
            moved = dot_nn(late1, w[t, 1, 0, :, n * 256 : (n + 1) * 256])
            for b in range(2):
                cols = slice(n * 256 + b * 128, n * 256 + b * 128 + 128)
                dn = moved[:, b * 128 : b * 128 + 128].astype(BF16).astype(F32)
                hat = (xs[2 * t + 1, :, cols].astype(F32) - mean1) * rstd1
                step = rstd1 * (dn * gain_blocks(ax.at[t], 1, 2 * n + b, 1) - one1 - hat * two1)
                dy0[:, cols] = (dy[:, cols].astype(F32) + step).astype(BF16)

        @pl.when(t > 0)
        def _():
            one0, two0 = row_means(late0, 0)
            mean0, rstd0 = stat[2 * t, 0], stat[2 * t, 1]
            for n in range(7):
                moved = dot_nn(late0, w[t, 0, 0, :, n * 256 : (n + 1) * 256])
                for b in range(2):
                    cols = slice(n * 256 + b * 128, n * 256 + b * 128 + 128)
                    dn = moved[:, b * 128 : b * 128 + 128].astype(BF16).astype(F32)
                    hat = (xs[2 * t, :, cols].astype(F32) - mean0) * rstd0
                    step = rstd0 * (dn * gain_blocks(ax.at[t], 0, 2 * n + b, 1) - one0 - hat * two0)
                    out = (dy0[:, cols].astype(F32) + step).astype(BF16).astype(F32)
                    dy[:, cols] = scaled_value(out).astype(BF16)

    def r0_copy(t):
        return remote(g.at[t, :, :, other_half], cr.at[t], r0_send.at[t], r0_recv.at[t], sibling)

    def r1_copy(t, d):
        there = (xx + d) % 4
        return remote(
            hs.at[t, there // 2, there % 2], xr.at[t, 3 - d], r1_send.at[t, d - 1], r1_recv.at[t, 3 - d], x_peer(d)
        )

    def r1_start(t):
        r0_copy(t).wait_recv()
        for l in range(2):
            for kind in range(2):
                hs[t, l, kind] = (g[t, l, kind, half, :].astype(F32) + cr[t, l, kind].astype(F32)).astype(BF16)
        for d in range(1, 4):
            r1_copy(t, d).start()

    def r2_copy(t, d):
        there = (z + d) % 8
        return remote(
            ks.at[t, there], zr.at[t, 7 - d], r2_send.at[t, d - 1], r2_recv.at[t, 7 - d], z_peer(d)
        )

    def r2_start(t):
        for d in range(1, 4):
            remote(xr.at[t, d - 1], xr.at[t, d - 1], r1_send.at[t, 0], r1_recv.at[t, d - 1], sibling).wait_recv()
        for k in range(8):
            begin_at = k * SUB // 128 * 128
            shift = k * SUB - begin_at
            width = -(-(shift + SUB) // 128) * 128
            cols = slice(begin_at, begin_at + width)
            total = hs[t, w_layer, w_kind, :, cols].astype(F32)
            for d in range(3):
                total = total + xr[t, d, :, cols].astype(F32)
            if shift:
                total = pltpu.roll(total, width - shift, 1)
            ks[t, k] = total[:, :256].astype(BF16)
        for d in range(1, 8):
            r2_copy(t, d).start()

    def r3_copy(t):
        return remote(fs.at[t], orr.at[rep % 8], r3_send.at[t], r3_recv.at[rep % 8], home(t))

    def r3_start(t):
        total = ks[t, z].astype(F32)
        for d in range(7):
            remote(zr.at[t, d], zr.at[t, d], r2_send.at[t, 0], r2_recv.at[t, d], sibling).wait_recv()
            total = total + zr[t, d].astype(F32)
        fs[t] = total.astype(BF16)

        @pl.when(is_home(t))
        def _():
            orr[rep % 8] = fs[t]

        @pl.when(jnp.logical_not(is_home(t)))
        def _():
            r3_copy(t).start()

    def backward(k, carry):
        t = SECTIONS - 1 - k
        par = k % 2

        def within(first):
            return jnp.logical_and(k >= first, k < SECTIONS + first)

        pl.when(k < SECTIONS)(lambda: begin(t, par))

        @pl.when(within(1))
        def _():
            gradients(t + 1)
            r0_copy(t + 1).start()

        pl.when(within(2))(lambda: r1_start(t + 2))
        pl.when(within(3))(lambda: r2_start(t + 3))
        pl.when(within(4))(lambda: r3_start(t + 4))
        pl.when(k < SECTIONS)(lambda: finish(t, par))
        return carry

    lax.fori_loop(0, SECTIONS + 4, backward, 0)

    for q in range(8):
        source_rep = (source_z % 4) * 8 + q
        here = jnp.logical_and(zl * 2 + source_z // 4 == sec, source_rep == rep)

        @pl.when(jnp.logical_not(here))
        def _(q=q):
            remote(orr.at[q], orr.at[q], r3_send.at[0], r3_recv.at[q], sibling).wait_recv()

    for l in range(2):
        for part in range(2):
            rows = slice(part * 32, (part + 1) * 32)
            out_d[l, rows, :] = orr[l * 4 + part][:, :SUB]
            out_u[l, rows, :] = orr[l * 4 + 2 + part][:, :SUB]

    y_weights(lambda copy: copy.wait_send())
    y_aux(lambda copy: copy.wait_send())
    y_memories(lambda copy: copy.wait_send())
    exchange_sent(back, 0)
    exchange_sent(back, 1)

    def drain(t, carry):
        @pl.when(t % 2 == zh)
        def _():
            zw_copy(t).wait_send()

            @pl.when(t < SECTIONS - 1)
            def _():
                zs_copy(t).wait_send()

            @pl.when(t > 0)
            def _():
                zr_copy(t).wait_send()

        @pl.when(t != sec)
        def _():
            for d in range(1, 4):
                w2_copy(t, d).wait_send()
            w3_copy(t).wait_send()

        r0_copy(t).wait_send()
        for d in range(1, 4):
            r1_copy(t, d).wait_send()
        for d in range(1, 8):
            r2_copy(t, d).wait_send()

        @pl.when(jnp.logical_not(is_home(t)))
        def _():
            r3_copy(t).wait_send()

        return carry

    lax.fori_loop(0, SECTIONS, drain, 0)


def local(inputs, cotangent, send_memory, recv_memory, sample_ids, gains, down_weight, up_weight):
    dwt = jnp.swapaxes(down_weight, 2, 3)
    gain = gains[0].astype(F32)
    rows = jnp.swapaxes(gain.reshape(2, 4, BLOCKS, 128), 0, 1).reshape(4, 2 * BLOCKS, 128)
    rows = jnp.pad(rows, ((0, 0), (0, 4), (0, 0)))

    anywhere = pl.BlockSpec(memory_space=pl.ANY)
    vmem = pl.BlockSpec(memory_space=pltpu.VMEM)
    sem = pltpu.SemaphoreType.DMA
    grad_down, grad_up = pl.pallas_call(
        kernel,
        out_shape=(
            jax.ShapeDtypeStruct((2, RANK, SUB), BF16),
            jax.ShapeDtypeStruct((2, RANK, SUB), BF16),
        ),
        in_specs=[pl.BlockSpec(memory_space=pltpu.SMEM)] + [anywhere] * 7,
        out_specs=(vmem, vmem),
        scratch_shapes=[
            pltpu.VMEM((8, 2, 2, RANK, SHARD), BF16),
            pltpu.VMEM((8, 8, 16, SHARD), BF16),
            pltpu.VMEM((8, 8, 16, SHARD), BF16),
            pltpu.VMEM((8, 32, 128), F32),
            pltpu.VMEM((8, 8, 128), F32),
            pltpu.VMEM((8, RANK, 128), BF16),
            pltpu.VMEM((8, 128), F32),
            pltpu.VMEM((RANK, 128), BF16),
            pltpu.VMEM((4, 32, 128), F32),
            pltpu.VMEM((2, 3 * RANK, SHARD), BF16),
            pltpu.VMEM((16, TOKENS, SHARD), BF16),
            pltpu.VMEM((TOKENS, SHARD), BF16),
            pltpu.VMEM((TOKENS, SHARD), BF16),
            pltpu.VMEM((TOKENS, SHARD), BF16),
            pltpu.VMEM((8, 16, SHARD), BF16),
            pltpu.VMEM((8, 16, SHARD), BF16),
            pltpu.VMEM((2, 4, TOKENS, 256), BF16),
            pltpu.VMEM((2, 4, TOKENS, 128), BF16),
            pltpu.VMEM((16, TOKENS, RANK), F32),
            pltpu.VMEM((16, TOKENS, RANK), BF16),
            pltpu.VMEM((16, 2, TOKENS, 128), F32),
            pltpu.VMEM((8, TOKENS, RANK), F32),
            pltpu.VMEM((2, TOKENS, RANK), BF16),
            pltpu.VMEM((2, TOKENS, RANK), F32),
            pltpu.VMEM((8, 2, 2, RANK, SHARD), BF16),
            pltpu.VMEM((8, 2, 2, 32, SHARD), BF16),
            pltpu.VMEM((8, 2, 2, 32, SHARD), BF16),
            pltpu.VMEM((8, 3, 32, SHARD), BF16),
            pltpu.VMEM((8, 8, 32, 256), BF16),
            pltpu.VMEM((8, 7, 32, 256), BF16),
            pltpu.VMEM((8, 32, 256), BF16),
            pltpu.VMEM((8, 32, 256), BF16),
            sem((15,)),
            sem((3, 5)),
            sem((7, 3)),
            sem((8,)),
            sem((8, 3)),
            sem((8, 2)),
            sem((8, 2)),
            sem((8,)),
            sem((8,)),
            sem((8,)),
            sem((8, 3)),
            sem((8, 4)),
            sem((8,)),
            sem((8,)),
            sem((2, 3)),
            sem((2, 4)),
            sem((2, 3)),
            sem((2, 4)),
            sem((8,)),
            sem((8,)),
            sem((8, 3)),
            sem((8, 3)),
            sem((8, 7)),
            sem((8, 7)),
            sem((8,)),
            sem((8,)),
        ],
        compiler_params=pltpu.CompilerParams(
            collective_id=0, has_side_effects=True, vmem_limit_bytes=56 * 1024 * 1024
        ),
        name="relay",
    )(sample_ids, inputs, cotangent, send_memory, recv_memory, dwt, up_weight, rows)

    start = lax.axis_index("dp") * SUB
    own_down = lax.dynamic_slice_in_dim(dwt[0], start, SUB, 2).astype(F32)
    own_gain = lax.dynamic_slice_in_dim(gain, start, SUB, 1)
    grad_gain = jnp.sum(own_down * grad_down.astype(F32), axis=1) / own_gain
    return (
        jnp.swapaxes(grad_down, 1, 2)[None],
        grad_up[None],
        grad_gain.astype(BF16)[None],
    )


def solution(mesh):
    in_specs = (
        P("dp", None, None, None),
        P("dp", None, None, None),
        P("section", "dp", None, None, None),
        P("section", "dp", None, None, None),
        P("dp", None),
        P("section", None, None),
        P("section", None, None, None),
        P("section", None, None, None),
    )
    out_specs = (
        P("section", None, "dp", None),
        P("section", None, None, "dp"),
        P("section", None, "dp"),
    )
    return jax.shard_map(local, mesh=mesh, in_specs=in_specs, out_specs=out_specs, check_vma=False)
```

```python
import functools
import math

import jax
import jax.numpy as jnp
from jax import lax
from jax.experimental import pallas as pl
from jax.experimental.pallas import tpu as pltpu
from jax.sharding import PartitionSpec as P

MESH = pl.DeviceIdType.MESH
F32 = jnp.float32
BF16 = jnp.bfloat16
EPSILON = 1e-05
SQUARE_EPS = 1e-06
D = 7168
RANK = 64
SHARD = 1792
BLOCKS = 14
TOKENS = 64
SECTIONS = 8
SUB = 224
ROOT = math.sqrt(2.0 / math.pi)
CUBE = 0.044715


def dot_nn(a, b):
    return lax.dot_general(a, b, (((1,), (0,)), ((), ())), preferred_element_type=F32)


def dot_nt(a, b):
    return lax.dot_general(a, b, (((1,), (1,)), ((), ())), preferred_element_type=F32)


def dot_tn(a, b):
    return lax.dot_general(a, b, (((0,), (0,)), ((), ())), preferred_element_type=F32)


def scaled_value(v):
    square = jnp.mean(v * v, axis=-1, keepdims=True)
    factor = (2.0 * jnp.sqrt(square + SQUARE_EPS)).astype(BF16).astype(F32)
    symbols = jnp.clip(v * (1.0 / factor), -1.0, 1.0).astype(BF16).astype(F32)
    return symbols * factor


def kernel(
    ids, inp, cot, snd, rcv, dwt, upw, gains, out_d, out_u, out_g,
    w, ms, mr, ax, px, pv, px_own, pv_own, all_gains, all_wide, ax_wide, own_down, rw, xs, xg, dy, dy0, inv, cov, msg, msb,
    pre_s, hid_s, stat, far_s, dpre_s, gp_s,
    g, cr, hs, xr, ks, zr, fs, orr,
    loc_sem, own_send, ax_send, w1_recv, wz_recv, ax_recv, ms_recv, mr_recv, zw_send, zs_send, zr_send, w2_send, w2_recv, w3_send, w3_recv,
    msg_send, msg_recv, msb_send, msb_recv, r0_send, r0_recv, r1_send, r1_recv, r2_send, r2_recv, r3_send, r3_recv,
):
    sec = lax.axis_index("section")
    rep = lax.axis_index("dp")
    y = sec // 2
    zh = sec % 2
    zl = rep // 8
    xx = (rep // 2) % 4
    co = rep % 2
    z = zh * 4 + zl
    w_layer = xx // 2
    w_kind = xx % 2
    half = pl.ds(pl.multiple_of(co * 32, 32), 32)
    other_half = pl.ds(pl.multiple_of((1 - co) * 32, 32), 32)
    sibling = {"dp": rep + 1 - 2 * co}
    home_x = z // 2
    home_core = z % 2

    def columns(at):
        return pl.ds(pl.multiple_of(at * SHARD, 128), SHARD)

    def remote(src, dst, send, recv, where):
        return pltpu.make_async_remote_copy(
            src_ref=src, dst_ref=dst, send_sem=send, recv_sem=recv, device_id=where, device_id_type=MESH
        )

    def x_peer(d):
        return {"dp": zl * 8 + ((xx + d) % 4) * 2 + co}

    def z_peer(d):
        other = (z + d) % 8
        return {"section": y * 2 + other // 4, "dp": (other % 4) * 8 + xx * 2 + co}

    def home(t):
        return {"section": t, "dp": y * 8 + home_x * 2 + home_core}

    def is_home(t):
        return jnp.logical_and(t == sec, y * 8 + home_x * 2 + home_core == rep)

    mine = columns(y)
    local = [
        pltpu.make_async_copy(inp.at[0, :, :, mine], inv, loc_sem.at[0]),
        pltpu.make_async_copy(cot.at[0, :, :, mine], cov, loc_sem.at[1]),
        pltpu.make_async_copy(dwt.at[0, :, :, mine], w.at[sec, :, 0], loc_sem.at[2]),
        pltpu.make_async_copy(upw.at[0, :, :, mine], w.at[sec, :, 1], loc_sem.at[3]),
        pltpu.make_async_copy(snd.at[0, 0, :, :, mine], ms.at[sec], loc_sem.at[4]),
        pltpu.make_async_copy(rcv.at[0, 0, :, :, mine], mr.at[sec], loc_sem.at[5]),
    ]
    for j in range(4):
        cols = slice(j * SHARD, (j + 1) * SHARD)
        local.append(pltpu.make_async_copy(dwt.at[0, :, :, cols], g.at[j, :, 0], loc_sem.at[6 + 2 * j]))
        local.append(pltpu.make_async_copy(upw.at[0, :, :, cols], g.at[j, :, 1], loc_sem.at[7 + 2 * j]))
    for copy in local:
        copy.start()

    barrier = pltpu.get_barrier_semaphore()

    def tell(where):
        pl.semaphore_signal(barrier, inc=1, device_id=where, device_id_type=MESH)

    for d in range(1, 8):
        tell({"section": (sec + d) % 8})
        tell(z_peer(d))
    for d in range(1, 4):
        tell(x_peer(d))
    tell(sibling)
    source_z = xx * 2 + co
    for q in range(8):
        source_section = zl * 2 + source_z // 4
        source_rep = (source_z % 4) * 8 + q
        here = jnp.logical_and(source_section == sec, source_rep == rep)

        @pl.when(jnp.logical_not(here))
        def _():
            tell({"section": source_section, "dp": source_rep})

    home_is_mine = y * 8 + home_x * 2 + home_core == rep
    pl.semaphore_wait(barrier, 7 + 7 + 3 + 1 + 8 - home_is_mine.astype(jnp.int32))

    own_slots = pl.ds(zh * 4, 4)
    far_slots = pl.ds(4 - zh * 4, 4)
    across = {"section": y * 2 + 1 - zh}

    def y_copy(d, kind):
        t2 = ((y + d) % 4) * 2 + zh
        there = columns((y + d) % 4)
        where = {"section": t2}
        if kind == 0:
            return remote(
                dwt.at[0, w_layer, half, there], w.at[sec, w_layer, 0, half], own_send.at[d - 1, 0], w1_recv.at[sec], where
            )
        if kind == 1:
            return remote(
                upw.at[0, w_layer, half, there], w.at[sec, w_layer, 1, half], own_send.at[d - 1, 0], w1_recv.at[sec], where
            )
        slots, number = (far_slots, 0) if kind in (2, 3) else (own_slots, 1)
        if kind in (2, 4):
            return remote(
                rcv.at[0, 0, slots, :, there], mr.at[sec, slots], own_send.at[d - 1, kind - 1], mr_recv.at[sec, number], where
            )
        return remote(
            snd.at[0, 0, slots, :, there], ms.at[sec, slots], own_send.at[d - 1, kind - 1], ms_recv.at[sec, number], where
        )

    def own_across(i):
        slot = pl.ds(4 - zh * 4 + i, 1)

        @pl.when(sec < SECTIONS - 1)
        def _():
            remote(snd.at[0, 0, slot, :, mine], ms.at[sec, slot], zs_send.at[sec], ms_recv.at[sec, 1], across).start()

        @pl.when(sec > 0)
        def _():
            remote(rcv.at[0, 0, slot, :, mine], mr.at[sec, slot], zr_send.at[sec], mr_recv.at[sec, 1], across).start()

    def aux_copies(d):
        t2 = (sec + d) % 8
        where = {"section": t2}
        return (
            remote(all_gains.at[t2 // 2], ax.at[sec], ax_send.at[d - 1, 0], ax_recv.at[sec, 0], where),
            remote(px_own, px.at[sec], ax_send.at[d - 1, 1], ax_recv.at[sec, 1], where),
            remote(pv_own, pv.at[sec], ax_send.at[d - 1, 2], ax_recv.at[sec, 2], where),
        )

    def y_weights(action):
        def some(kind):
            for d in (1, 3, 2):
                action(y_copy(d, kind))

        pl.when(w_kind == 0)(lambda: some(0))
        pl.when(w_kind == 1)(lambda: some(1))

    def y_memories(action):
        def some(kind):
            for d in (1, 3, 2):
                action(y_copy(d, kind))

        for kind in range(2, 6):
            pl.when(sec > 0 if kind % 2 == 0 else sec < SECTIONS - 1)(functools.partial(some, kind))

    def y_aux(action):
        for d in range(1, 8):
            for copy in aux_copies(d):
                action(copy)

    y_weights(lambda copy: copy.start())
    plain = gains[...].astype(F32)
    for j in range(4):
        rows = [
            plain[l : l + 1, j * SHARD + b * 128 : j * SHARD + b * 128 + 128] for l in range(2) for b in range(BLOCKS)
        ]
        all_wide[j] = jnp.concatenate(rows + [jnp.ones((4, 128), F32)], axis=0)
        all_gains[j] = all_wide[j].astype(BF16)
    for copy in local:
        copy.wait()

    def gain_blocks(rows_ref, l, first, count):
        rows = [rows_ref[l * BLOCKS + b : l * BLOCKS + b + 1, :] for b in range(first, first + count)]
        return jnp.concatenate(rows, axis=-1) if count > 1 else rows[0]

    def fold(weights, rows_ref, into):
        for l in range(2):
            gained = weights[l, 0].astype(F32) * gain_blocks(rows_ref, l, 0, BLOCKS)
            into[l * RANK : (l + 1) * RANK, :] = gained.astype(BF16)
        into[2 * RANK :, :] = weights[0, 1]

    ones = jnp.ones((16, SHARD), BF16)
    products = jnp.zeros((RANK, 2 * RANK), F32)
    up_sum = jnp.zeros((RANK, 16), F32)
    whole = jnp.zeros((16, 3 * RANK), F32)
    for j in range(4):
        fold(g.at[j], all_wide.at[j], rw.at[0])
        here_sums = dot_nt(ones, rw[0])
        whole = whole + here_sums
        px_own[2 * j : 2 * j + 1, :] = here_sums[:1, : 2 * RANK]
        px_own[2 * j + 1 : 2 * j + 2, :] = jnp.concatenate([here_sums[:1, 2 * RANK :], jnp.zeros((1, RANK), F32)], axis=-1)
        up = rw[0, 2 * RANK :, :]
        products = products + dot_nt(up, rw[0, RANK:, :])
        up_sum = up_sum + dot_nt(up, ones)
    products = products - up_sum[:, :1] * (whole[:1, RANK:] * (1.0 / D))
    pv_own[...] = products.astype(BF16)
    ax[sec] = all_gains[y]
    px[sec] = px_own[...]
    pv[sec] = pv_own[...]
    y_aux(lambda copy: copy.start())
    y_memories(lambda copy: copy.start())

    slice_at = SUB * (xx * 2 + co)
    block_at = jnp.minimum(slice_at // 128, BLOCKS - 3)
    turn = (384 - (slice_at - block_at * 128)) % 384
    for l in range(2):
        window = g[zl, l, 0, :, pl.ds(pl.multiple_of(block_at * 128, 128), 384)].astype(F32)
        own_down[l] = pltpu.roll(window, turn, 1)[:, :256]
    own_gain = []
    for l in range(2):
        rows = [all_wide[zl, pl.ds(l * BLOCKS + block_at + i, 1), :] for i in range(3)]
        rows = jnp.broadcast_to(jnp.concatenate(rows, axis=-1), (8, 384))
        own_gain.append(pltpu.roll(rows, turn, 1)[:1, :256])

    for i in range(4):
        slot = zh * 4 + i
        place = jnp.int32(0)
        for m in range(8):
            place = jnp.where(ids[0, m] == slot, m, place)
        xs[0, i * 16 : (i + 1) * 16, :] = inv[place]
        dy[i * 16 : (i + 1) * 16, :] = cov[place]

    def w_part(t, kind_x):
        return w.at[t, kind_x // 2, kind_x % 2, half]

    def w2_copy(t, d):
        return remote(w_part(t, xx), w_part(t, xx), w2_send.at[t, d - 1], w2_recv.at[t, xx], x_peer(d))

    def zw_copy(t, piece):
        part = w.at[t, w_layer, w_kind, half, pl.ds(piece * (SHARD // 2), SHARD // 2)]
        return remote(part, part, zw_send.at[t, piece], wz_recv.at[t, piece], z_peer(7 if piece else 1))

    def zw_sends(t, piece):
        near = t % 2 == zh
        if piece:
            return jnp.logical_or(jnp.logical_and(near, zl == 0), jnp.logical_and(jnp.logical_not(near), zl > 0))
        return jnp.logical_or(jnp.logical_and(near, zl == 3), jnp.logical_and(jnp.logical_not(near), zl < 3))

    def zs_copy(t):
        return remote(ms.at[t, far_slots], ms.at[t, far_slots], zs_send.at[t], ms_recv.at[t, 1], across)

    def zr_copy(t):
        return remote(mr.at[t, far_slots], mr.at[t, far_slots], zr_send.at[t], mr_recv.at[t, 1], across)

    def ms_wait(t, number):
        slots = own_slots if number else far_slots

        @pl.when(t != sec)
        def _():
            remote(ms.at[t, slots], ms.at[t, slots], zs_send.at[t], ms_recv.at[t, number], sibling).wait_recv()

    def mr_wait(t, number):
        slots = own_slots if number else far_slots

        @pl.when(t != sec)
        def _():
            remote(mr.at[t, slots], mr.at[t, slots], zr_send.at[t], mr_recv.at[t, number], sibling).wait_recv()

    def relay(b):
        @pl.when(jnp.logical_and(b % 2 == zh, b != sec))
        def _():
            ms_wait(b, 0)
            zs_copy(b).start()

        @pl.when(jnp.logical_and(b % 2 != zh, b + 1 != sec))
        def _():
            mr_wait(b + 1, 0)
            zr_copy(b + 1).start()

    def along_z(t, piece):
        pl.when(zw_sends(t, piece))(lambda: zw_copy(t, piece).start())

    def over_x(t):
        for d in range(1, 4):
            w2_copy(t, d).start()

    def near_weights(i, carry):
        t = 2 * i + zh

        @pl.when(t != sec)
        def _():
            remote(w_part(t, xx), w_part(t, xx), own_send.at[0, 0], w1_recv.at[t], sibling).wait_recv()

        along_z(t, 0)
        along_z(t, 1)
        pl.when(t != sec)(lambda: over_x(t))
        return carry

    def far_weights(piece, early):
        def take(i, carry):
            t = 2 * i + 1 - zh
            zw_copy(t, piece).wait_recv()
            along_z(t, piece)
            if not early:
                over_x(t)
            return carry

        lax.fori_loop(0, 4, take, 0)

    def w3_copy(t):
        return remote(w.at[t, :, :, half], w.at[t, :, :, half], w3_send.at[t], w3_recv.at[t], sibling)

    def w3_arrival(t):
        return remote(w.at[t, :, :, other_half], w.at[t, :, :, other_half], w3_send.at[t], w3_recv.at[t], sibling)

    def pass_to_core(t):
        @pl.when(t != sec)
        def _():
            for d in range(1, 4):
                source = (xx + d) % 4
                remote(w_part(t, source), w_part(t, source), w2_send.at[t, 0], w2_recv.at[t, source], sibling).wait_recv()
            w3_copy(t).start()

    def exchange_copy(buffers, par, d):
        held, send, recv = buffers
        return remote(
            held.at[par, y], held.at[par, y], send.at[par, d - 1], recv.at[par, y], {"section": ((y + d) % 4) * 2 + zh}
        )

    def exchange_start(buffers, par, value):
        buffers[0][par, y] = value
        for d in (2, 1, 3):
            exchange_copy(buffers, par, d).start()

    def exchange_sent(buffers, par):
        for d in range(1, 4):
            exchange_copy(buffers, par, d).wait_send()

    def exchange_wait(buffers, par):
        held, send, recv = buffers
        for d in range(1, 4):
            source = (y + d) % 4
            remote(
                held.at[par, source], held.at[par, source], send.at[par, d - 1], recv.at[par, source], sibling
            ).wait_recv()

    ahead = (msg, msg_send, msg_recv)
    back = (msb, msb_send, msb_recv)

    def sums_of(t, j):
        return px[t, 2 * j : 2 * j + 1, :], px[t, 2 * j + 1 : 2 * j + 2, :RANK]

    def gelu(pre):
        return (0.5 * pre * (1.0 + jnp.tanh(ROOT * (pre + CUBE * pre * pre * pre)))).astype(BF16)

    def gelu_slope(pre):
        tanh = jnp.tanh(ROOT * (pre + CUBE * pre * pre * pre))
        return 0.5 * (1.0 + tanh) + 0.5 * pre * (1.0 - tanh * tanh) * ROOT * (1.0 + 3.0 * CUBE * pre * pre)

    def ready(t):
        @pl.when(t != sec)
        def _():
            w3_arrival(t).wait_recv()
            for n, held in enumerate((ax, px, pv)):
                remote(held.at[t], held.at[t], ax_send.at[0, n], ax_recv.at[t, n], sibling).wait_recv()

        ax_wide[t] = ax[t].astype(F32)
        fold(w.at[t], ax_wide.at[t], rw.at[t % 2])

    for i in range(4):
        own_across(i)
    lax.fori_loop(0, 4, near_weights, 0)

    @pl.when(zl < 2)
    def _():
        far_weights(0, True)
        far_weights(1, False)

    @pl.when(zl >= 2)
    def _():
        far_weights(1, True)
        far_weights(0, False)

    def relays(b, carry):
        relay(b)
        return carry

    lax.fori_loop(0, SECTIONS - 1, relays, 0)
    pass_to_core(0)
    pass_to_core(1)
    ready(0)

    def wide(column):
        return jnp.broadcast_to(column, (TOKENS, 128))

    def forward(t, carry):
        at = 2 * t
        par = t % 2
        centres, spreads = [], []
        for i in range(4):
            rows = slice(i * 16, (i + 1) * 16)
            xv = xs[at, rows, :].astype(F32)
            centre = jnp.sum(xv, axis=-1, keepdims=True) * (1.0 / SHARD)
            moved = xv - centre
            spreads.append(jnp.sum(moved * moved, axis=-1, keepdims=True))
            centres.append(centre)
            xg[rows, :] = moved.astype(BF16)
        centre = jnp.concatenate(centres, axis=0)
        spread = jnp.concatenate(spreads, axis=0)
        part = dot_nt(xg[...], rw[par])
        lane = lax.broadcasted_iota(jnp.int32, (TOKENS, RANK), 1)
        packed = jnp.zeros((TOKENS, RANK), F32)
        for start, number in ((0, centre), (3, spread)):
            rest = number
            for step in range(3):
                piece = rest.astype(BF16).astype(F32)
                packed = jnp.where(lane == start + step, piece, packed)
                rest = rest - piece

        pl.when(t > 1)(lambda: exchange_sent(ahead, par))
        exchange_start(ahead, par, jnp.concatenate([part, packed], axis=-1).astype(BF16))

        pl.when(t < SECTIONS - 2)(lambda: pass_to_core(t + 2))
        pl.when(t < SECTIONS - 1)(lambda: ready(t + 1))

        exchange_wait(ahead, par)
        first = jnp.zeros((TOKENS, 2 * RANK), F32)
        second = jnp.zeros((TOKENS, 2 * RANK), F32)
        means = []
        spread = jnp.zeros((TOKENS, 1), F32)
        for j in range(4):
            first = first + msg[par, j, :, : 2 * RANK].astype(F32)
            got = msg[par, j, :, 2 * RANK :].astype(F32)
            second = second + got
            means.append(got[:, 64:65] + got[:, 65:66] + got[:, 66:67])
            spread = spread + (got[:, 67:68] + got[:, 68:69] + got[:, 69:70])
        mean = 0.25 * (means[0] + means[1] + means[2] + means[3])
        second = second[:, :RANK]
        up_mean = jnp.zeros((1, RANK), F32)
        for j in range(4):
            apart = means[j] - mean
            spread = spread + SHARD * (apart * apart)
            sums, up_sums = sums_of(t, j)
            first = first + apart * sums
            second = second + apart * up_sums
            up_mean = up_mean + up_sums * (1.0 / D)
        rstd = lax.rsqrt(spread * (1.0 / D) + EPSILON)
        pre = first[:, :RANK] * rstd
        hidden = gelu(pre)
        moved = dot_nn(hidden, pv[t])
        hidden_wide = hidden.astype(F32)
        far = second + moved[:, RANK:]
        spread1 = jnp.maximum(spread + jnp.sum(hidden_wide * (second + far), axis=-1, keepdims=True), 0.0)
        rstd1 = lax.rsqrt(spread1 * (1.0 / D) + EPSILON)
        mean1 = mean + jnp.sum(hidden_wide * up_mean, axis=-1, keepdims=True)
        pre1 = (first[:, RANK:] + moved[:, :RANK]) * rstd1
        hidden1 = gelu(pre1)
        pre_s[at] = pre
        pre_s[at + 1] = pre1
        hid_s[at] = hidden
        hid_s[at + 1] = hidden1
        far_s[t] = far
        stat[at, 0] = wide(mean)
        stat[at, 1] = wide(rstd)
        stat[at + 1, 0] = wide(mean1)
        stat[at + 1, 1] = wide(rstd1)

        def next_layer(n):
            cols = slice(n * 256, (n + 1) * 256)
            branch = dot_nn(hidden, w[t, 0, 1, :, cols])
            middle = (xs[at, :, cols].astype(F32) + branch).astype(BF16)
            xs[at + 1, :, cols] = middle
            return middle

        @pl.when(t == SECTIONS - 1)
        def _():
            for n in range(7):
                next_layer(n)

        @pl.when(t < SECTIONS - 1)
        def _():
            ms_wait(t, 1)
            mr_wait(t + 1, 1)
            for n in range(7):
                middle = next_layer(n).astype(F32)
                branch = dot_nn(hidden1, w[t, 1, 1, :, n * 256 : (n + 1) * 256])
                out = (middle + branch).astype(BF16).astype(F32)
                for b in range(2):
                    cols = slice(n * 256 + b * 128, n * 256 + b * 128 + 128)
                    old = ms[t, own_slots, :, cols].reshape(TOKENS, 128).astype(F32)
                    kept = mr[t + 1, own_slots, :, cols].reshape(TOKENS, 128).astype(F32)
                    value = scaled_value(out[:, b * 128 : b * 128 + 128] - old)
                    xs[at + 2, :, cols] = (kept + value).astype(BF16)

        return carry

    lax.fori_loop(0, SECTIONS, forward, 0)
    exchange_sent(ahead, 0)
    exchange_sent(ahead, 1)

    def begin(t, par):
        part = dot_nt(dy[...], w[t, :, 1].reshape(2 * RANK, SHARD))
        pl.when(t < SECTIONS - 2)(lambda: exchange_sent(back, par))
        exchange_start(back, par, part.astype(BF16))
        gp_s[0] = gelu_slope(pre_s[2 * t])
        gp_s[1] = gelu_slope(pre_s[2 * t + 1])
        hidden = hid_s[2 * t + 1]
        for n in range(7):
            cols = slice(n * 256, (n + 1) * 256)
            g[t, 1, 1, :, cols] = dot_tn(hidden, dy[:, cols]).astype(BF16)

    def gradients(t):
        hidden = hid_s[2 * t]
        for n in range(7):
            cols = slice(n * 256, (n + 1) * 256)
            for l in range(2):
                at = 2 * t + l
                pieces = []
                for b in (2 * n, 2 * n + 1):
                    part = xs[at, :, b * 128 : (b + 1) * 128].astype(F32)
                    pieces.append((part - stat[at, 0]) * stat[at, 1] * gain_blocks(ax_wide.at[t], l, b, 1))
                normed = jnp.concatenate(pieces, axis=-1).astype(BF16)
                g[t, l, 0, :, cols] = dot_tn(dpre_s[l], normed).astype(BF16)
            g[t, 0, 1, :, cols] = dot_tn(hidden, dy0[:, cols]).astype(BF16)

    def finish(t, par):
        exchange_wait(back, par)
        total = jnp.zeros((TOKENS, 2 * RANK), F32)
        for j in range(4):
            total = total + msb[par, j].astype(F32)
        both_sums = px[t, 0:1, :] + px[t, 2:3, :] + px[t, 4:5, :] + px[t, 6:7, :]

        def row_means(late, l):
            numbers = late.astype(F32)
            one = jnp.sum(numbers * both_sums[:, l * RANK : (l + 1) * RANK], axis=-1, keepdims=True) * (1.0 / D)
            two = jnp.sum(numbers * pre_s[2 * t + l], axis=-1, keepdims=True) * (1.0 / D)
            return one, two

        late1 = (total[:, RANK:].astype(BF16).astype(F32) * gp_s[1]).astype(BF16)
        dpre_s[1] = late1
        one1, two1 = row_means(late1, 1)
        mean1, rstd1 = stat[2 * t + 1, 0], stat[2 * t + 1, 1]
        column = rstd1[:, :RANK]
        inner = total[:, :RANK] + column * (dot_nt(late1, pv[t, :, :RANK]) - two1 * column * far_s[t])
        late0 = (inner.astype(BF16).astype(F32) * gp_s[0]).astype(BF16)
        dpre_s[0] = late0
        for n in range(7):
            moved = dot_nn(late1, w[t, 1, 0, :, n * 256 : (n + 1) * 256])
            for b in range(2):
                cols = slice(n * 256 + b * 128, n * 256 + b * 128 + 128)
                dn = moved[:, b * 128 : b * 128 + 128].astype(BF16).astype(F32)
                hat = (xs[2 * t + 1, :, cols].astype(F32) - mean1) * rstd1
                step = rstd1 * (dn * gain_blocks(ax_wide.at[t], 1, 2 * n + b, 1) - one1 - hat * two1)
                dy0[:, cols] = (dy[:, cols].astype(F32) + step).astype(BF16)

        @pl.when(t > 0)
        def _():
            one0, two0 = row_means(late0, 0)
            mean0, rstd0 = stat[2 * t, 0], stat[2 * t, 1]
            for n in range(7):
                moved = dot_nn(late0, w[t, 0, 0, :, n * 256 : (n + 1) * 256])
                for b in range(2):
                    cols = slice(n * 256 + b * 128, n * 256 + b * 128 + 128)
                    dn = moved[:, b * 128 : b * 128 + 128].astype(BF16).astype(F32)
                    hat = (xs[2 * t, :, cols].astype(F32) - mean0) * rstd0
                    step = rstd0 * (dn * gain_blocks(ax_wide.at[t], 0, 2 * n + b, 1) - one0 - hat * two0)
                    out = (dy0[:, cols].astype(F32) + step).astype(BF16).astype(F32)
                    dy[:, cols] = scaled_value(out).astype(BF16)

    def r0_copy(t):
        return remote(g.at[t, :, :, other_half], cr.at[t], r0_send.at[t], r0_recv.at[t], sibling)

    def r1_copy(t, d):
        there = (xx + d) % 4
        return remote(
            hs.at[t, there // 2, there % 2], xr.at[t, 3 - d], r1_send.at[t, d - 1], r1_recv.at[t, 3 - d], x_peer(d)
        )

    def r1_start(t):
        r0_copy(t).wait_recv()
        for l in range(2):
            for kind in range(2):
                hs[t, l, kind] = g[t, l, kind, half, :] + cr[t, l, kind]
        for d in range(1, 4):
            r1_copy(t, d).start()

    def r2_copy(t, d):
        there = (z + d) % 8
        return remote(
            ks.at[t, there], zr.at[t, 7 - d], r2_send.at[t, d - 1], r2_recv.at[t, 7 - d], z_peer(d)
        )

    def r2_start(t):
        for d in range(1, 4):
            remote(xr.at[t, d - 1], xr.at[t, d - 1], r1_send.at[t, 0], r1_recv.at[t, d - 1], sibling).wait_recv()
        for k in range(8):
            begin_at = k * SUB // 128 * 128
            shift = k * SUB - begin_at
            width = -(-(shift + SUB) // 128) * 128
            cols = slice(begin_at, begin_at + width)
            total = hs[t, w_layer, w_kind, :, cols].astype(F32)
            for d in range(3):
                total = total + xr[t, d, :, cols].astype(F32)
            if shift:
                total = pltpu.roll(total, width - shift, 1)
            ks[t, k] = total[:, :256].astype(BF16)
        for d in range(1, 8):
            r2_copy(t, d).start()

    def r3_copy(t):
        return remote(fs.at[t], orr.at[rep % 8], r3_send.at[t], r3_recv.at[rep % 8], home(t))

    def r3_start(t):
        total = ks[t, z].astype(F32)
        for d in range(7):
            remote(zr.at[t, d], zr.at[t, d], r2_send.at[t, 0], r2_recv.at[t, d], sibling).wait_recv()
            total = total + zr[t, d].astype(F32)
        fs[t] = total.astype(BF16)

        @pl.when(is_home(t))
        def _():
            orr[rep % 8] = fs[t]

        @pl.when(jnp.logical_not(is_home(t)))
        def _():
            r3_copy(t).start()

    def backward(k, carry):
        t = SECTIONS - 1 - k
        par = k % 2

        def within(first):
            return jnp.logical_and(k >= first, k < SECTIONS + first)

        pl.when(k < SECTIONS)(lambda: begin(t, par))

        @pl.when(within(1))
        def _():
            gradients(t + 1)
            r0_copy(t + 1).start()

        pl.when(within(3))(lambda: r2_start(t + 3))
        pl.when(within(5))(lambda: r3_start(t + 5))
        pl.when(k < SECTIONS)(lambda: finish(t, par))
        pl.when(within(1))(lambda: r1_start(t + 1))
        return carry

    lax.fori_loop(0, SECTIONS + 5, backward, 0)

    for q in range(8):
        source_rep = (source_z % 4) * 8 + q
        here = jnp.logical_and(zl * 2 + source_z // 4 == sec, source_rep == rep)

        @pl.when(jnp.logical_not(here))
        def _(q=q):
            remote(orr.at[q], orr.at[q], r3_send.at[0], r3_recv.at[q], sibling).wait_recv()

    for l in range(2):
        for part in range(2):
            rows = slice(part * 32, (part + 1) * 32)
            out_d[l, rows, :] = orr[l * 4 + part][:, :SUB]
            out_u[l, rows, :] = orr[l * 4 + 2 + part][:, :SUB]
        along = jnp.zeros((1, 256), F32)
        for part in range(2):
            along = along + jnp.sum(
                own_down[l, part * 32 : part * 32 + 32, :] * orr[l * 4 + part].astype(F32), axis=0, keepdims=True
            )
        out_g[l : l + 1, :] = (along / own_gain[l])[:, :SUB]

    y_weights(lambda copy: copy.wait_send())
    y_aux(lambda copy: copy.wait_send())
    y_memories(lambda copy: copy.wait_send())
    exchange_sent(back, 0)
    exchange_sent(back, 1)

    def drain(t, carry):
        for piece in range(2):
            pl.when(zw_sends(t, piece))(functools.partial(lambda piece: zw_copy(t, piece).wait_send(), piece))

        @pl.when(t % 2 == zh)
        def _():
            @pl.when(t < SECTIONS - 1)
            def _():
                zs_copy(t).wait_send()

            @pl.when(t > 0)
            def _():
                zr_copy(t).wait_send()

        @pl.when(t != sec)
        def _():
            for d in range(1, 4):
                w2_copy(t, d).wait_send()
            w3_copy(t).wait_send()

        r0_copy(t).wait_send()
        for d in range(1, 4):
            r1_copy(t, d).wait_send()
        for d in range(1, 8):
            r2_copy(t, d).wait_send()

        @pl.when(jnp.logical_not(is_home(t)))
        def _():
            r3_copy(t).wait_send()

        return carry

    lax.fori_loop(0, SECTIONS, drain, 0)


def local(inputs, cotangent, send_memory, recv_memory, sample_ids, gains, down_weight, up_weight):
    dwt = jnp.swapaxes(down_weight, 2, 3)
    anywhere = pl.BlockSpec(memory_space=pl.ANY)
    vmem = pl.BlockSpec(memory_space=pltpu.VMEM)
    sem = pltpu.SemaphoreType.DMA
    grad_down, grad_up, grad_gain = pl.pallas_call(
        kernel,
        out_shape=(
            jax.ShapeDtypeStruct((2, RANK, SUB), BF16),
            jax.ShapeDtypeStruct((2, RANK, SUB), BF16),
            jax.ShapeDtypeStruct((2, SUB), F32),
        ),
        in_specs=[pl.BlockSpec(memory_space=pltpu.SMEM)] + [anywhere] * 6 + [vmem],
        out_specs=(vmem, vmem, vmem),
        scratch_shapes=[
            pltpu.VMEM((8, 2, 2, RANK, SHARD), BF16),
            pltpu.VMEM((8, 8, 16, SHARD), BF16),
            pltpu.VMEM((8, 8, 16, SHARD), BF16),
            pltpu.VMEM((8, 32, 128), BF16),
            pltpu.VMEM((8, 8, 128), F32),
            pltpu.VMEM((8, RANK, 128), BF16),
            pltpu.VMEM((8, 128), F32),
            pltpu.VMEM((RANK, 128), BF16),
            pltpu.VMEM((4, 32, 128), BF16),
            pltpu.VMEM((4, 32, 128), F32),
            pltpu.VMEM((8, 32, 128), F32),
            pltpu.VMEM((2, RANK, 256), F32),
            pltpu.VMEM((2, 3 * RANK, SHARD), BF16),
            pltpu.VMEM((16, TOKENS, SHARD), BF16),
            pltpu.VMEM((TOKENS, SHARD), BF16),
            pltpu.VMEM((TOKENS, SHARD), BF16),
            pltpu.VMEM((TOKENS, SHARD), BF16),
            pltpu.VMEM((8, 16, SHARD), BF16),
            pltpu.VMEM((8, 16, SHARD), BF16),
            pltpu.VMEM((2, 4, TOKENS, 256), BF16),
            pltpu.VMEM((2, 4, TOKENS, 128), BF16),
            pltpu.VMEM((16, TOKENS, RANK), F32),
            pltpu.VMEM((16, TOKENS, RANK), BF16),
            pltpu.VMEM((16, 2, TOKENS, 128), F32),
            pltpu.VMEM((8, TOKENS, RANK), F32),
            pltpu.VMEM((2, TOKENS, RANK), BF16),
            pltpu.VMEM((2, TOKENS, RANK), F32),
            pltpu.VMEM((8, 2, 2, RANK, SHARD), BF16),
            pltpu.VMEM((8, 2, 2, 32, SHARD), BF16),
            pltpu.VMEM((8, 2, 2, 32, SHARD), BF16),
            pltpu.VMEM((8, 3, 32, SHARD), BF16),
            pltpu.VMEM((8, 8, 32, 256), BF16),
            pltpu.VMEM((8, 7, 32, 256), BF16),
            pltpu.VMEM((8, 32, 256), BF16),
            pltpu.VMEM((8, 32, 256), BF16),
            sem((14,)),
            sem((3, 5)),
            sem((7, 3)),
            sem((8,)),
            sem((8, 2)),
            sem((8, 3)),
            sem((8, 2)),
            sem((8, 2)),
            sem((8, 2)),
            sem((8,)),
            sem((8,)),
            sem((8, 3)),
            sem((8, 4)),
            sem((8,)),
            sem((8,)),
            sem((2, 3)),
            sem((2, 4)),
            sem((2, 3)),
            sem((2, 4)),
            sem((8,)),
            sem((8,)),
            sem((8, 3)),
            sem((8, 3)),
            sem((8, 7)),
            sem((8, 7)),
            sem((8,)),
            sem((8,)),
        ],
        compiler_params=pltpu.CompilerParams(
            collective_id=0, has_side_effects=True, vmem_limit_bytes=56 * 1024 * 1024
        ),
        name="relay",
    )(sample_ids, inputs, cotangent, send_memory, recv_memory, dwt, up_weight, gains[0])

    return (
        jnp.swapaxes(grad_down, 1, 2)[None],
        grad_up[None],
        grad_gain.astype(BF16)[None],
    )


def solution(mesh):
    in_specs = (
        P("dp", None, None, None),
        P("dp", None, None, None),
        P("section", "dp", None, None, None),
        P("section", "dp", None, None, None),
        P("dp", None),
        P("section", None, None),
        P("section", None, None, None),
        P("section", None, None, None),
    )
    out_specs = (
        P("section", None, "dp", None),
        P("section", None, None, "dp"),
        P("section", None, "dp"),
    )
    return jax.shard_map(local, mesh=mesh, in_specs=in_specs, out_specs=out_specs, check_vma=False)
```

```python
import functools
import math

import jax
import jax.numpy as jnp
from jax import lax
from jax.experimental import pallas as pl
from jax.experimental.pallas import tpu as pltpu
from jax.sharding import PartitionSpec as P

MESH = pl.DeviceIdType.MESH
F32 = jnp.float32
BF16 = jnp.bfloat16
EPSILON = 1e-05
SQUARE_EPS = 1e-06
D = 7168
RANK = 64
SHARD = 1792
BLOCKS = 14
TOKENS = 64
SECTIONS = 8
SUB = 224
ROOT = math.sqrt(2.0 / math.pi)
CUBE = 0.044715


def dot_nn(a, b):
    return lax.dot_general(a, b, (((1,), (0,)), ((), ())), preferred_element_type=F32)


def dot_nt(a, b):
    return lax.dot_general(a, b, (((1,), (1,)), ((), ())), preferred_element_type=F32)


def dot_tn(a, b):
    return lax.dot_general(a, b, (((0,), (0,)), ((), ())), preferred_element_type=F32)


def scaled_value(v):
    square = jnp.mean(v * v, axis=-1, keepdims=True)
    factor = (2.0 * jnp.sqrt(square + SQUARE_EPS)).astype(BF16).astype(F32)
    symbols = jnp.clip(v * (1.0 / factor), -1.0, 1.0).astype(BF16).astype(F32)
    return symbols * factor


def kernel(
    ids, inp, cot, snd, rcv, dwt, upw, gains, out_d, out_u, out_g,
    w, ms, mr, ax, px, pv, px_own, pv_own, all_gains, all_wide, ax_wide, own_down, rw, xs, xg, dy, dy0, inv, cov, msg, msb,
    pre_s, hid_s, stat, far_s, dpre_s, gp_s,
    g, cr, hs, xr, ks, zr, fs, orr,
    loc_sem, own_send, ax_send, w1_recv, wz_recv, ax_recv, ms_recv, mr_recv, zw_send, zs_send, zr_send, w2_send, w2_recv, w3_send, w3_recv,
    msg_send, msg_recv, msb_send, msb_recv, r0_send, r0_recv, r1_send, r1_recv, r2_send, r2_recv, r3_send, r3_recv,
):
    sec = lax.axis_index("section")
    rep = lax.axis_index("dp")
    y = sec // 2
    zh = sec % 2
    zl = rep // 8
    xx = (rep // 2) % 4
    co = rep % 2
    z = zh * 4 + zl
    w_layer = xx // 2
    w_kind = xx % 2
    half = pl.ds(pl.multiple_of(co * 32, 32), 32)
    other_half = pl.ds(pl.multiple_of((1 - co) * 32, 32), 32)
    sibling = {"dp": rep + 1 - 2 * co}
    home_x = z // 2
    home_core = z % 2

    def columns(at):
        return pl.ds(pl.multiple_of(at * SHARD, 128), SHARD)

    def remote(src, dst, send, recv, where):
        return pltpu.make_async_remote_copy(
            src_ref=src, dst_ref=dst, send_sem=send, recv_sem=recv, device_id=where, device_id_type=MESH
        )

    def x_peer(d):
        return {"dp": zl * 8 + ((xx + d) % 4) * 2 + co}

    def z_peer(d):
        other = (z + d) % 8
        return {"section": y * 2 + other // 4, "dp": (other % 4) * 8 + xx * 2 + co}

    def home(t):
        return {"section": t, "dp": y * 8 + home_x * 2 + home_core}

    def is_home(t):
        return jnp.logical_and(t == sec, y * 8 + home_x * 2 + home_core == rep)

    mine = columns(y)
    local = [
        pltpu.make_async_copy(inp.at[0, :, :, mine], inv, loc_sem.at[0]),
        pltpu.make_async_copy(cot.at[0, :, :, mine], cov, loc_sem.at[1]),
        pltpu.make_async_copy(dwt.at[0, :, :, mine], w.at[sec, :, 0], loc_sem.at[2]),
        pltpu.make_async_copy(upw.at[0, :, :, mine], w.at[sec, :, 1], loc_sem.at[3]),
        pltpu.make_async_copy(snd.at[0, 0, :, :, mine], ms.at[sec], loc_sem.at[4]),
        pltpu.make_async_copy(rcv.at[0, 0, :, :, mine], mr.at[sec], loc_sem.at[5]),
    ]
    for j in range(4):
        cols = slice(j * SHARD, (j + 1) * SHARD)
        local.append(pltpu.make_async_copy(dwt.at[0, :, :, cols], g.at[j, :, 0], loc_sem.at[6 + 2 * j]))
        local.append(pltpu.make_async_copy(upw.at[0, :, :, cols], g.at[j, :, 1], loc_sem.at[7 + 2 * j]))
    for copy in local[6:] + local[:6]:
        copy.start()

    barrier = pltpu.get_barrier_semaphore()

    def tell(where):
        pl.semaphore_signal(barrier, inc=1, device_id=where, device_id_type=MESH)

    for d in range(1, 8):
        tell({"section": (sec + d) % 8})
        tell(z_peer(d))
    for d in range(1, 4):
        tell(x_peer(d))
    tell(sibling)
    source_z = xx * 2 + co
    for q in range(8):
        source_section = zl * 2 + source_z // 4
        source_rep = (source_z % 4) * 8 + q
        here = jnp.logical_and(source_section == sec, source_rep == rep)

        @pl.when(jnp.logical_not(here))
        def _():
            tell({"section": source_section, "dp": source_rep})

    home_is_mine = y * 8 + home_x * 2 + home_core == rep
    pl.semaphore_wait(barrier, 7 + 7 + 3 + 1 + 8 - home_is_mine.astype(jnp.int32))

    own_slots = pl.ds(zh * 4, 4)
    far_slots = pl.ds(4 - zh * 4, 4)
    across = {"section": y * 2 + 1 - zh}

    def y_copy(d, kind):
        t2 = ((y + d) % 4) * 2 + zh
        there = columns((y + d) % 4)
        where = {"section": t2}
        if kind == 0:
            return remote(
                dwt.at[0, w_layer, half, there], w.at[sec, w_layer, 0, half], own_send.at[d - 1, 0], w1_recv.at[sec], where
            )
        if kind == 1:
            return remote(
                upw.at[0, w_layer, half, there], w.at[sec, w_layer, 1, half], own_send.at[d - 1, 0], w1_recv.at[sec], where
            )
        slots, number = (far_slots, 0) if kind in (2, 3) else (own_slots, 1)
        if kind in (2, 4):
            return remote(
                rcv.at[0, 0, slots, :, there], mr.at[sec, slots], own_send.at[d - 1, kind - 1], mr_recv.at[sec, number], where
            )
        return remote(
            snd.at[0, 0, slots, :, there], ms.at[sec, slots], own_send.at[d - 1, kind - 1], ms_recv.at[sec, number], where
        )

    def own_across(i):
        slot = pl.ds(4 - zh * 4 + i, 1)

        @pl.when(sec < SECTIONS - 1)
        def _():
            remote(snd.at[0, 0, slot, :, mine], ms.at[sec, slot], zs_send.at[sec], ms_recv.at[sec, 1], across).start()

        @pl.when(sec > 0)
        def _():
            remote(rcv.at[0, 0, slot, :, mine], mr.at[sec, slot], zr_send.at[sec], mr_recv.at[sec, 1], across).start()

    def aux_copies(d):
        t2 = (sec + d) % 8
        where = {"section": t2}
        return (
            remote(all_gains.at[t2 // 2], ax.at[sec], ax_send.at[d - 1, 0], ax_recv.at[sec, 0], where),
            remote(px_own, px.at[sec], ax_send.at[d - 1, 1], ax_recv.at[sec, 1], where),
            remote(pv_own, pv.at[sec], ax_send.at[d - 1, 2], ax_recv.at[sec, 2], where),
        )

    def y_weights(action):
        def some(kind):
            for d in (1, 3, 2):
                action(y_copy(d, kind))

        pl.when(w_kind == 0)(lambda: some(0))
        pl.when(w_kind == 1)(lambda: some(1))

    def y_memories(action):
        def some(kind):
            for d in (1, 3, 2):
                action(y_copy(d, kind))

        for kind in range(2, 6):
            pl.when(sec > 0 if kind % 2 == 0 else sec < SECTIONS - 1)(functools.partial(some, kind))

    def y_aux(action):
        for d in range(1, 8):
            for copy in aux_copies(d):
                action(copy)

    y_weights(lambda copy: copy.start())
    for i in range(4):
        own_across(i)
    plain = gains[...].astype(F32)
    for j in range(4):
        rows = [
            plain[l : l + 1, j * SHARD + b * 128 : j * SHARD + b * 128 + 128] for l in range(2) for b in range(BLOCKS)
        ]
        all_wide[j] = jnp.concatenate(rows + [jnp.ones((4, 128), F32)], axis=0)
        all_gains[j] = all_wide[j].astype(BF16)
    for copy in local[6:]:
        copy.wait()

    def gain_blocks(rows_ref, l, first, count):
        rows = [rows_ref[l * BLOCKS + b : l * BLOCKS + b + 1, :] for b in range(first, first + count)]
        return jnp.concatenate(rows, axis=-1) if count > 1 else rows[0]

    def fold(weights, rows_ref, into):
        for l in range(2):
            gained = weights[l, 0].astype(F32) * gain_blocks(rows_ref, l, 0, BLOCKS)
            into[l * RANK : (l + 1) * RANK, :] = gained.astype(BF16)
        into[2 * RANK :, :] = weights[0, 1]

    ones = jnp.ones((16, SHARD), BF16)
    products = jnp.zeros((RANK, 2 * RANK), F32)
    up_sum = jnp.zeros((RANK, 16), F32)
    whole = jnp.zeros((16, 3 * RANK), F32)
    for j in range(4):
        fold(g.at[j], all_wide.at[j], rw.at[0])
        here_sums = dot_nt(ones, rw[0])
        whole = whole + here_sums
        px_own[2 * j : 2 * j + 1, :] = here_sums[:1, : 2 * RANK]
        px_own[2 * j + 1 : 2 * j + 2, :] = jnp.concatenate([here_sums[:1, 2 * RANK :], jnp.zeros((1, RANK), F32)], axis=-1)
        up = rw[0, 2 * RANK :, :]
        products = products + dot_nt(up, rw[0, RANK:, :])
        up_sum = up_sum + dot_nt(up, ones)
    products = products - up_sum[:, :1] * (whole[:1, RANK:] * (1.0 / D))
    pv_own[...] = products.astype(BF16)
    ax[sec] = all_gains[y]
    px[sec] = px_own[...]
    pv[sec] = pv_own[...]
    y_aux(lambda copy: copy.start())
    y_memories(lambda copy: copy.start())
    for copy in local[:6]:
        copy.wait()

    slice_at = SUB * (xx * 2 + co)
    block_at = jnp.minimum(slice_at // 128, BLOCKS - 3)
    turn = (384 - (slice_at - block_at * 128)) % 384
    for l in range(2):
        window = g[zl, l, 0, :, pl.ds(pl.multiple_of(block_at * 128, 128), 384)].astype(F32)
        own_down[l] = pltpu.roll(window, turn, 1)[:, :256]
    own_gain = []
    for l in range(2):
        rows = [all_wide[zl, pl.ds(l * BLOCKS + block_at + i, 1), :] for i in range(3)]
        rows = jnp.broadcast_to(jnp.concatenate(rows, axis=-1), (8, 384))
        own_gain.append(pltpu.roll(rows, turn, 1)[:1, :256])

    for i in range(4):
        slot = zh * 4 + i
        place = jnp.int32(0)
        for m in range(8):
            place = jnp.where(ids[0, m] == slot, m, place)
        xs[0, i * 16 : (i + 1) * 16, :] = inv[place]
        dy[i * 16 : (i + 1) * 16, :] = cov[place]

    def w_part(t, kind_x):
        return w.at[t, kind_x // 2, kind_x % 2, half]

    def w2_copy(t, d):
        return remote(w_part(t, xx), w_part(t, xx), w2_send.at[t, d - 1], w2_recv.at[t, xx], x_peer(d))

    def zw_copy(t, piece):
        part = w.at[t, w_layer, w_kind, half, pl.ds(piece * (SHARD // 2), SHARD // 2)]
        return remote(part, part, zw_send.at[t, piece], wz_recv.at[t, piece], z_peer(7 if piece else 1))

    def zw_sends(t, piece):
        near = t % 2 == zh
        if piece:
            return jnp.logical_or(jnp.logical_and(near, zl == 0), jnp.logical_and(jnp.logical_not(near), zl > 0))
        return jnp.logical_or(jnp.logical_and(near, zl == 3), jnp.logical_and(jnp.logical_not(near), zl < 3))

    def zs_copy(t):
        return remote(ms.at[t, far_slots], ms.at[t, far_slots], zs_send.at[t], ms_recv.at[t, 1], across)

    def zr_copy(t):
        return remote(mr.at[t, far_slots], mr.at[t, far_slots], zr_send.at[t], mr_recv.at[t, 1], across)

    def ms_wait(t, number):
        slots = own_slots if number else far_slots

        @pl.when(t != sec)
        def _():
            remote(ms.at[t, slots], ms.at[t, slots], zs_send.at[t], ms_recv.at[t, number], sibling).wait_recv()

    def mr_wait(t, number):
        slots = own_slots if number else far_slots

        @pl.when(t != sec)
        def _():
            remote(mr.at[t, slots], mr.at[t, slots], zr_send.at[t], mr_recv.at[t, number], sibling).wait_recv()

    def relay(b):
        @pl.when(jnp.logical_and(b % 2 == zh, b != sec))
        def _():
            ms_wait(b, 0)
            zs_copy(b).start()

        @pl.when(jnp.logical_and(b % 2 != zh, b + 1 != sec))
        def _():
            mr_wait(b + 1, 0)
            zr_copy(b + 1).start()

    def along_z(t, piece):
        pl.when(zw_sends(t, piece))(lambda: zw_copy(t, piece).start())

    def over_x(t):
        for d in range(1, 4):
            w2_copy(t, d).start()

    def near_weights(i, carry):
        t = 2 * i + zh

        @pl.when(t != sec)
        def _():
            remote(w_part(t, xx), w_part(t, xx), own_send.at[0, 0], w1_recv.at[t], sibling).wait_recv()

        along_z(t, 0)
        along_z(t, 1)
        pl.when(t != sec)(lambda: over_x(t))
        return carry

    def far_weights(piece, early):
        def take(i, carry):
            t = 2 * i + 1 - zh
            zw_copy(t, piece).wait_recv()
            along_z(t, piece)
            if not early:
                over_x(t)
            return carry

        lax.fori_loop(0, 4, take, 0)

    def w3_copy(t):
        return remote(w.at[t, :, :, half], w.at[t, :, :, half], w3_send.at[t], w3_recv.at[t], sibling)

    def w3_arrival(t):
        return remote(w.at[t, :, :, other_half], w.at[t, :, :, other_half], w3_send.at[t], w3_recv.at[t], sibling)

    def pass_to_core(t):
        @pl.when(t != sec)
        def _():
            for d in range(1, 4):
                source = (xx + d) % 4
                remote(w_part(t, source), w_part(t, source), w2_send.at[t, 0], w2_recv.at[t, source], sibling).wait_recv()
            w3_copy(t).start()

    def exchange_copy(buffers, par, d):
        held, send, recv = buffers
        return remote(
            held.at[par, y], held.at[par, y], send.at[par, d - 1], recv.at[par, y], {"section": ((y + d) % 4) * 2 + zh}
        )

    def exchange_start(buffers, par, value):
        buffers[0][par, y] = value
        for d in (2, 1, 3):
            exchange_copy(buffers, par, d).start()

    def exchange_sent(buffers, par):
        for d in range(1, 4):
            exchange_copy(buffers, par, d).wait_send()

    def exchange_wait(buffers, par):
        held, send, recv = buffers
        for d in range(1, 4):
            source = (y + d) % 4
            remote(
                held.at[par, source], held.at[par, source], send.at[par, d - 1], recv.at[par, source], sibling
            ).wait_recv()

    ahead = (msg, msg_send, msg_recv)
    back = (msb, msb_send, msb_recv)

    def sums_of(t, j):
        return px[t, 2 * j : 2 * j + 1, :], px[t, 2 * j + 1 : 2 * j + 2, :RANK]

    def gelu(pre):
        return (0.5 * pre * (1.0 + jnp.tanh(ROOT * (pre + CUBE * pre * pre * pre)))).astype(BF16)

    def gelu_slope(pre):
        tanh = jnp.tanh(ROOT * (pre + CUBE * pre * pre * pre))
        return 0.5 * (1.0 + tanh) + 0.5 * pre * (1.0 - tanh * tanh) * ROOT * (1.0 + 3.0 * CUBE * pre * pre)

    def ready(t):
        @pl.when(t != sec)
        def _():
            w3_arrival(t).wait_recv()
            for n, held in enumerate((ax, px, pv)):
                remote(held.at[t], held.at[t], ax_send.at[0, n], ax_recv.at[t, n], sibling).wait_recv()

        ax_wide[t] = ax[t].astype(F32)
        fold(w.at[t], ax_wide.at[t], rw.at[t % 2])

    lax.fori_loop(0, 4, near_weights, 0)

    @pl.when(zl < 2)
    def _():
        far_weights(0, True)
        far_weights(1, False)

    @pl.when(zl >= 2)
    def _():
        far_weights(1, True)
        far_weights(0, False)

    def relays(b, carry):
        relay(b)
        return carry

    lax.fori_loop(0, SECTIONS - 1, relays, 0)
    pass_to_core(0)
    pass_to_core(1)
    ready(0)

    def send_back(t, par):
        part = dot_nt(dy[...], w[t, :, 1].reshape(2 * RANK, SHARD))
        exchange_start(back, par, part.astype(BF16))

    def wide(column):
        return jnp.broadcast_to(column, (TOKENS, 128))

    def forward(t, carry):
        at = 2 * t
        par = t % 2
        centres, spreads = [], []
        for i in range(4):
            rows = slice(i * 16, (i + 1) * 16)
            xv = xs[at, rows, :].astype(F32)
            centre = jnp.sum(xv, axis=-1, keepdims=True) * (1.0 / SHARD)
            moved = xv - centre
            spreads.append(jnp.sum(moved * moved, axis=-1, keepdims=True))
            centres.append(centre)
            xg[rows, :] = moved.astype(BF16)
        centre = jnp.concatenate(centres, axis=0)
        spread = jnp.concatenate(spreads, axis=0)
        part = dot_nt(xg[...], rw[par])
        lane = lax.broadcasted_iota(jnp.int32, (TOKENS, RANK), 1)
        packed = jnp.zeros((TOKENS, RANK), F32)
        for start, number in ((0, centre), (3, spread)):
            rest = number
            for step in range(3):
                piece = rest.astype(BF16).astype(F32)
                packed = jnp.where(lane == start + step, piece, packed)
                rest = rest - piece

        pl.when(t > 1)(lambda: exchange_sent(ahead, par))
        exchange_start(ahead, par, jnp.concatenate([part, packed], axis=-1).astype(BF16))

        pl.when(t == SECTIONS - 1)(lambda: send_back(t, 0))
        pl.when(t < SECTIONS - 2)(lambda: pass_to_core(t + 2))
        pl.when(t < SECTIONS - 1)(lambda: ready(t + 1))

        exchange_wait(ahead, par)
        first = jnp.zeros((TOKENS, 2 * RANK), F32)
        second = jnp.zeros((TOKENS, 2 * RANK), F32)
        means = []
        spread = jnp.zeros((TOKENS, 1), F32)
        for j in range(4):
            first = first + msg[par, j, :, : 2 * RANK].astype(F32)
            got = msg[par, j, :, 2 * RANK :].astype(F32)
            second = second + got
            means.append(got[:, 64:65] + got[:, 65:66] + got[:, 66:67])
            spread = spread + (got[:, 67:68] + got[:, 68:69] + got[:, 69:70])
        mean = 0.25 * (means[0] + means[1] + means[2] + means[3])
        second = second[:, :RANK]
        up_mean = jnp.zeros((1, RANK), F32)
        for j in range(4):
            apart = means[j] - mean
            spread = spread + SHARD * (apart * apart)
            sums, up_sums = sums_of(t, j)
            first = first + apart * sums
            second = second + apart * up_sums
            up_mean = up_mean + up_sums * (1.0 / D)
        rstd = lax.rsqrt(spread * (1.0 / D) + EPSILON)
        pre = first[:, :RANK] * rstd
        hidden = gelu(pre)
        moved = dot_nn(hidden, pv[t])
        hidden_wide = hidden.astype(F32)
        far = second + moved[:, RANK:]
        spread1 = jnp.maximum(spread + jnp.sum(hidden_wide * (second + far), axis=-1, keepdims=True), 0.0)
        rstd1 = lax.rsqrt(spread1 * (1.0 / D) + EPSILON)
        mean1 = mean + jnp.sum(hidden_wide * up_mean, axis=-1, keepdims=True)
        pre1 = (first[:, RANK:] + moved[:, :RANK]) * rstd1
        hidden1 = gelu(pre1)
        pre_s[at] = pre
        pre_s[at + 1] = pre1
        hid_s[at] = hidden
        hid_s[at + 1] = hidden1
        far_s[t] = far
        stat[at, 0] = wide(mean)
        stat[at, 1] = wide(rstd)
        stat[at + 1, 0] = wide(mean1)
        stat[at + 1, 1] = wide(rstd1)

        def next_layer(n):
            cols = slice(n * 256, (n + 1) * 256)
            branch = dot_nn(hidden, w[t, 0, 1, :, cols])
            middle = (xs[at, :, cols].astype(F32) + branch).astype(BF16)
            xs[at + 1, :, cols] = middle
            return middle

        @pl.when(t == SECTIONS - 1)
        def _():
            for n in range(7):
                next_layer(n)

        @pl.when(t < SECTIONS - 1)
        def _():
            ms_wait(t, 1)
            mr_wait(t + 1, 1)
            for n in range(7):
                middle = next_layer(n).astype(F32)
                branch = dot_nn(hidden1, w[t, 1, 1, :, n * 256 : (n + 1) * 256])
                out = (middle + branch).astype(BF16).astype(F32)
                for b in range(2):
                    cols = slice(n * 256 + b * 128, n * 256 + b * 128 + 128)
                    old = ms[t, own_slots, :, cols].reshape(TOKENS, 128).astype(F32)
                    kept = mr[t + 1, own_slots, :, cols].reshape(TOKENS, 128).astype(F32)
                    value = scaled_value(out[:, b * 128 : b * 128 + 128] - old)
                    xs[at + 2, :, cols] = (kept + value).astype(BF16)

        return carry

    lax.fori_loop(0, SECTIONS, forward, 0)
    exchange_sent(ahead, 0)
    exchange_sent(ahead, 1)

    def begin(t, par):
        @pl.when(t < SECTIONS - 1)
        def _():
            pl.when(t < SECTIONS - 2)(lambda: exchange_sent(back, par))
            send_back(t, par)

        gp_s[0] = gelu_slope(pre_s[2 * t])
        gp_s[1] = gelu_slope(pre_s[2 * t + 1])
        hidden = hid_s[2 * t + 1]
        for n in range(7):
            cols = slice(n * 256, (n + 1) * 256)
            g[t, 1, 1, :, cols] = dot_tn(hidden, dy[:, cols]).astype(BF16)

    def gradients(t):
        hidden = hid_s[2 * t]
        for n in range(7):
            cols = slice(n * 256, (n + 1) * 256)
            for l in range(2):
                at = 2 * t + l
                pieces = []
                for b in (2 * n, 2 * n + 1):
                    part = xs[at, :, b * 128 : (b + 1) * 128].astype(F32)
                    pieces.append((part - stat[at, 0]) * stat[at, 1] * gain_blocks(ax_wide.at[t], l, b, 1))
                normed = jnp.concatenate(pieces, axis=-1).astype(BF16)
                g[t, l, 0, :, cols] = dot_tn(dpre_s[l], normed).astype(BF16)
            g[t, 0, 1, :, cols] = dot_tn(hidden, dy0[:, cols]).astype(BF16)

    def finish(t, par):
        exchange_wait(back, par)
        total = jnp.zeros((TOKENS, 2 * RANK), F32)
        for j in range(4):
            total = total + msb[par, j].astype(F32)
        both_sums = px[t, 0:1, :] + px[t, 2:3, :] + px[t, 4:5, :] + px[t, 6:7, :]

        def row_means(late, l):
            numbers = late.astype(F32)
            one = jnp.sum(numbers * both_sums[:, l * RANK : (l + 1) * RANK], axis=-1, keepdims=True) * (1.0 / D)
            two = jnp.sum(numbers * pre_s[2 * t + l], axis=-1, keepdims=True) * (1.0 / D)
            return one, two

        late1 = (total[:, RANK:].astype(BF16).astype(F32) * gp_s[1]).astype(BF16)
        dpre_s[1] = late1
        one1, two1 = row_means(late1, 1)
        mean1, rstd1 = stat[2 * t + 1, 0], stat[2 * t + 1, 1]
        column = rstd1[:, :RANK]
        inner = total[:, :RANK] + column * (dot_nt(late1, pv[t, :, :RANK]) - two1 * column * far_s[t])
        late0 = (inner.astype(BF16).astype(F32) * gp_s[0]).astype(BF16)
        dpre_s[0] = late0
        for n in range(7):
            moved = dot_nn(late1, w[t, 1, 0, :, n * 256 : (n + 1) * 256])
            for b in range(2):
                cols = slice(n * 256 + b * 128, n * 256 + b * 128 + 128)
                dn = moved[:, b * 128 : b * 128 + 128].astype(BF16).astype(F32)
                hat = (xs[2 * t + 1, :, cols].astype(F32) - mean1) * rstd1
                step = rstd1 * (dn * gain_blocks(ax_wide.at[t], 1, 2 * n + b, 1) - one1 - hat * two1)
                dy0[:, cols] = (dy[:, cols].astype(F32) + step).astype(BF16)

        @pl.when(t > 0)
        def _():
            one0, two0 = row_means(late0, 0)
            mean0, rstd0 = stat[2 * t, 0], stat[2 * t, 1]
            for n in range(7):
                moved = dot_nn(late0, w[t, 0, 0, :, n * 256 : (n + 1) * 256])
                for b in range(2):
                    cols = slice(n * 256 + b * 128, n * 256 + b * 128 + 128)
                    dn = moved[:, b * 128 : b * 128 + 128].astype(BF16).astype(F32)
                    hat = (xs[2 * t, :, cols].astype(F32) - mean0) * rstd0
                    step = rstd0 * (dn * gain_blocks(ax_wide.at[t], 0, 2 * n + b, 1) - one0 - hat * two0)
                    out = (dy0[:, cols].astype(F32) + step).astype(BF16).astype(F32)
                    dy[:, cols] = scaled_value(out).astype(BF16)

    def r0_copy(t):
        return remote(g.at[t, :, :, other_half], cr.at[t], r0_send.at[t], r0_recv.at[t], sibling)

    def r1_copy(t, d):
        there = (xx + d) % 4
        return remote(
            hs.at[t, there // 2, there % 2], xr.at[t, 3 - d], r1_send.at[t, d - 1], r1_recv.at[t, 3 - d], x_peer(d)
        )

    def r1_start(t):
        r0_copy(t).wait_recv()
        for l in range(2):
            for kind in range(2):
                hs[t, l, kind] = g[t, l, kind, half, :] + cr[t, l, kind]
        for d in range(1, 4):
            r1_copy(t, d).start()

    def r2_copy(t, d):
        there = (z + d) % 8
        return remote(
            ks.at[t, there], zr.at[t, 7 - d], r2_send.at[t, d - 1], r2_recv.at[t, 7 - d], z_peer(d)
        )

    def r2_start(t):
        for d in range(1, 4):
            remote(xr.at[t, d - 1], xr.at[t, d - 1], r1_send.at[t, 0], r1_recv.at[t, d - 1], sibling).wait_recv()
        for k in range(8):
            begin_at = k * SUB // 128 * 128
            shift = k * SUB - begin_at
            width = -(-(shift + SUB) // 128) * 128
            cols = slice(begin_at, begin_at + width)
            total = hs[t, w_layer, w_kind, :, cols].astype(F32)
            for d in range(3):
                total = total + xr[t, d, :, cols].astype(F32)
            if shift:
                total = pltpu.roll(total, width - shift, 1)
            ks[t, k] = total[:, :256].astype(BF16)
        for d in range(1, 8):
            r2_copy(t, d).start()

    def r3_copy(t):
        return remote(fs.at[t], orr.at[rep % 8], r3_send.at[t], r3_recv.at[rep % 8], home(t))

    def r3_start(t):
        total = ks[t, z].astype(F32)
        for d in range(7):
            remote(zr.at[t, d], zr.at[t, d], r2_send.at[t, 0], r2_recv.at[t, d], sibling).wait_recv()
            total = total + zr[t, d].astype(F32)
        fs[t] = total.astype(BF16)

        @pl.when(is_home(t))
        def _():
            orr[rep % 8] = fs[t]

        @pl.when(jnp.logical_not(is_home(t)))
        def _():
            r3_copy(t).start()

    def backward(k, carry):
        t = SECTIONS - 1 - k
        par = k % 2

        def within(first):
            return jnp.logical_and(k >= first, k < SECTIONS + first)

        pl.when(k < SECTIONS)(lambda: begin(t, par))

        @pl.when(within(1))
        def _():
            gradients(t + 1)
            r0_copy(t + 1).start()

        pl.when(within(3))(lambda: r2_start(t + 3))
        pl.when(within(5))(lambda: r3_start(t + 5))
        pl.when(k < SECTIONS)(lambda: finish(t, par))
        pl.when(within(1))(lambda: r1_start(t + 1))
        return carry

    lax.fori_loop(0, SECTIONS + 5, backward, 0)

    for q in range(8):
        source_rep = (source_z % 4) * 8 + q
        here = jnp.logical_and(zl * 2 + source_z // 4 == sec, source_rep == rep)

        @pl.when(jnp.logical_not(here))
        def _(q=q):
            remote(orr.at[q], orr.at[q], r3_send.at[0], r3_recv.at[q], sibling).wait_recv()

    for l in range(2):
        for part in range(2):
            rows = slice(part * 32, (part + 1) * 32)
            out_d[l, rows, :] = orr[l * 4 + part][:, :SUB]
            out_u[l, rows, :] = orr[l * 4 + 2 + part][:, :SUB]
        along = jnp.zeros((1, 256), F32)
        for part in range(2):
            along = along + jnp.sum(
                own_down[l, part * 32 : part * 32 + 32, :] * orr[l * 4 + part].astype(F32), axis=0, keepdims=True
            )
        out_g[l : l + 1, :] = (along / own_gain[l])[:, :SUB]

    y_weights(lambda copy: copy.wait_send())
    y_aux(lambda copy: copy.wait_send())
    y_memories(lambda copy: copy.wait_send())
    exchange_sent(back, 0)
    exchange_sent(back, 1)

    def drain(t, carry):
        for piece in range(2):
            pl.when(zw_sends(t, piece))(functools.partial(lambda piece: zw_copy(t, piece).wait_send(), piece))

        @pl.when(t % 2 == zh)
        def _():
            @pl.when(t < SECTIONS - 1)
            def _():
                zs_copy(t).wait_send()

            @pl.when(t > 0)
            def _():
                zr_copy(t).wait_send()

        @pl.when(t != sec)
        def _():
            for d in range(1, 4):
                w2_copy(t, d).wait_send()
            w3_copy(t).wait_send()

        r0_copy(t).wait_send()
        for d in range(1, 4):
            r1_copy(t, d).wait_send()
        for d in range(1, 8):
            r2_copy(t, d).wait_send()

        @pl.when(jnp.logical_not(is_home(t)))
        def _():
            r3_copy(t).wait_send()

        return carry

    lax.fori_loop(0, SECTIONS, drain, 0)


def local(inputs, cotangent, send_memory, recv_memory, sample_ids, gains, down_weight, up_weight):
    dwt = jnp.swapaxes(down_weight, 2, 3)
    anywhere = pl.BlockSpec(memory_space=pl.ANY)
    vmem = pl.BlockSpec(memory_space=pltpu.VMEM)
    sem = pltpu.SemaphoreType.DMA
    grad_down, grad_up, grad_gain = pl.pallas_call(
        kernel,
        out_shape=(
            jax.ShapeDtypeStruct((2, RANK, SUB), BF16),
            jax.ShapeDtypeStruct((2, RANK, SUB), BF16),
            jax.ShapeDtypeStruct((2, SUB), F32),
        ),
        in_specs=[pl.BlockSpec(memory_space=pltpu.SMEM)] + [anywhere] * 6 + [vmem],
        out_specs=(vmem, vmem, vmem),
        scratch_shapes=[
            pltpu.VMEM((8, 2, 2, RANK, SHARD), BF16),
            pltpu.VMEM((8, 8, 16, SHARD), BF16),
            pltpu.VMEM((8, 8, 16, SHARD), BF16),
            pltpu.VMEM((8, 32, 128), BF16),
            pltpu.VMEM((8, 8, 128), F32),
            pltpu.VMEM((8, RANK, 128), BF16),
            pltpu.VMEM((8, 128), F32),
            pltpu.VMEM((RANK, 128), BF16),
            pltpu.VMEM((4, 32, 128), BF16),
            pltpu.VMEM((4, 32, 128), F32),
            pltpu.VMEM((8, 32, 128), F32),
            pltpu.VMEM((2, RANK, 256), F32),
            pltpu.VMEM((2, 3 * RANK, SHARD), BF16),
            pltpu.VMEM((16, TOKENS, SHARD), BF16),
            pltpu.VMEM((TOKENS, SHARD), BF16),
            pltpu.VMEM((TOKENS, SHARD), BF16),
            pltpu.VMEM((TOKENS, SHARD), BF16),
            pltpu.VMEM((8, 16, SHARD), BF16),
            pltpu.VMEM((8, 16, SHARD), BF16),
            pltpu.VMEM((2, 4, TOKENS, 256), BF16),
            pltpu.VMEM((2, 4, TOKENS, 128), BF16),
            pltpu.VMEM((16, TOKENS, RANK), F32),
            pltpu.VMEM((16, TOKENS, RANK), BF16),
            pltpu.VMEM((16, 2, TOKENS, 128), F32),
            pltpu.VMEM((8, TOKENS, RANK), F32),
            pltpu.VMEM((2, TOKENS, RANK), BF16),
            pltpu.VMEM((2, TOKENS, RANK), F32),
            pltpu.VMEM((8, 2, 2, RANK, SHARD), BF16),
            pltpu.VMEM((8, 2, 2, 32, SHARD), BF16),
            pltpu.VMEM((8, 2, 2, 32, SHARD), BF16),
            pltpu.VMEM((8, 3, 32, SHARD), BF16),
            pltpu.VMEM((8, 8, 32, 256), BF16),
            pltpu.VMEM((8, 7, 32, 256), BF16),
            pltpu.VMEM((8, 32, 256), BF16),
            pltpu.VMEM((8, 32, 256), BF16),
            sem((14,)),
            sem((3, 5)),
            sem((7, 3)),
            sem((8,)),
            sem((8, 2)),
            sem((8, 3)),
            sem((8, 2)),
            sem((8, 2)),
            sem((8, 2)),
            sem((8,)),
            sem((8,)),
            sem((8, 3)),
            sem((8, 4)),
            sem((8,)),
            sem((8,)),
            sem((2, 3)),
            sem((2, 4)),
            sem((2, 3)),
            sem((2, 4)),
            sem((8,)),
            sem((8,)),
            sem((8, 3)),
            sem((8, 3)),
            sem((8, 7)),
            sem((8, 7)),
            sem((8,)),
            sem((8,)),
        ],
        compiler_params=pltpu.CompilerParams(
            collective_id=0, has_side_effects=True, vmem_limit_bytes=56 * 1024 * 1024
        ),
        name="relay",
    )(sample_ids, inputs, cotangent, send_memory, recv_memory, dwt, up_weight, gains[0])

    return (
        jnp.swapaxes(grad_down, 1, 2)[None],
        grad_up[None],
        grad_gain.astype(BF16)[None],
    )


def solution(mesh):
    in_specs = (
        P("dp", None, None, None),
        P("dp", None, None, None),
        P("section", "dp", None, None, None),
        P("section", "dp", None, None, None),
        P("dp", None),
        P("section", None, None),
        P("section", None, None, None),
        P("section", None, None, None),
    )
    out_specs = (
        P("section", None, "dp", None),
        P("section", None, None, "dp"),
        P("section", None, "dp"),
    )
    return jax.shard_map(local, mesh=mesh, in_specs=in_specs, out_specs=out_specs, check_vma=False)
```
